32 devices in a mesh: dp: 8 (over y, x, core), mp: 4 (over z).
Axes of the slice: x: 2, y: 2, z: 4, core: 2. Of those that a mesh axis runs over, the one named last changes fastest.
Arguments:
- query_tokens: bfloat16 [8, 257, 5120], P('dp', None, 'mp'), may hold values from -200 to 200
- key_tokens: bfloat16 [8, 257, 5120], P('dp', None, 'mp'), may hold values from -6.5 to 6.5
- value_tokens: bfloat16 [8, 257, 5120], P('dp', None, 'mp'), may hold values from -6 to 6
- head_weight: bfloat16 [5120, 1024], P('mp', 'dp'), may hold values from -0.078125 to 0.078125
- image_cache: bfloat16 [256, 1024], P(('dp', 'mp')), may hold values from -6 to 6
- text_embed: bfloat16 [256, 1024], P(('dp', 'mp')), may hold values from -6 to 6
- text_pair: int32 [256], P(('dp', 'mp')), may hold values from 0 to 255, as said below
- image_group: int32 [256], P(('dp', 'mp')), may hold values from 0 to 127
- text_group: int32 [256], P(('dp', 'mp')), may hold values from 0 to 127
- logit_scale: float32 [], replicated, may hold values from 2.6 to 2.8
- logit_bias: float32 [], replicated, may hold values from -9 to -8
Outputs:
- query_grad: bfloat16 [8, 257, 5120], P('dp', None, 'mp')
- key_grad: bfloat16 [8, 257, 5120], P('dp', None, 'mp')
- value_grad: bfloat16 [8, 257, 5120], P('dp', None, 'mp')
- image_grad: float32 [256, 1024], P(('dp', 'mp'))
- text_grad: float32 [256, 1024], P(('dp', 'mp'))
- row_loss: float32 [256], P(('dp', 'mp'))
The draws below stay inside these ranges and needn't reach their ends.
Inputs may be any that keep to these rules, and one draw needn't show every extreme that they name: Text j is the caption of image text_pair[j]; every image has exactly one such text.
All inputs are finite; a program needn't handle non-finite values.
Results may differ from the reference program's by a relative error of at most 0.012.
Values may be sent and summed in bfloat16 or wider, within the bound.
A program may use at most 64 MiB of HBM per device.

```python
import math
import jax
import jax.numpy as jnp
from jax import lax

D = 5120
HEADS = 40
HEAD_DIM = 128
SEQ = 257
EMBED = 1024
IMAGES = 8
BLOCK = 32
PAIRS = 256


def shared_normals(key):
    return jnp.clip(jax.random.normal(key, (IMAGES, SEQ, D), jnp.float32), -6.0, 6.0)


def draw_key_tokens(key, part):
    planted = shared_normals(key)
    return planted.astype(jnp.bfloat16)


def draw_query_tokens(key, part):
    own_key = jax.random.fold_in(key, 5)
    queries = jnp.clip(jax.random.normal(own_key, (IMAGES, SEQ, D), jnp.float32), -6.0, 6.0)
    return queries.astype(jnp.bfloat16)


def cluster_parts(key):
    groups = max(PAIRS // 64, 1)
    pairing = jax.random.permutation(jax.random.fold_in(key, 101), PAIRS).astype(jnp.int32)
    member = jax.random.randint(jax.random.fold_in(key, 102), (PAIRS,), 0, groups).astype(jnp.int32)
    centres = jax.random.normal(jax.random.fold_in(key, 103), (groups, EMBED), jnp.float32)
    image_noise = jax.random.normal(jax.random.fold_in(key, 104), (PAIRS, EMBED), jnp.float32)
    return (pairing, member, centres, image_noise)


def mixed_rows(centre_rows, noise_rows, share):
    blended = math.sqrt(share) * centre_rows + math.sqrt(1.0 - share) * noise_rows
    return jnp.clip(blended, -6.0, 6.0)


def draw_text_pair(key, part):
    pairing, member, centres, image_noise = cluster_parts(key)
    return pairing


def draw_image_cache(key, part):
    pairing, member, centres, image_noise = cluster_parts(key)
    share = 0.5
    return mixed_rows(centres[member], image_noise, share).astype(jnp.bfloat16)


def draw_text_embed(key, part):
    pairing, member, centres, image_noise = cluster_parts(key)
    key = jax.random.fold_in(key, 22)
    own_noise = jax.random.normal(jax.random.fold_in(key, 1), (PAIRS, EMBED), jnp.float32)
    caption_noise = math.sqrt(0.6) * image_noise[pairing] + math.sqrt(0.4) * own_noise
    share = 0.5
    return mixed_rows(centres[member[pairing]], caption_noise, share).astype(jnp.bfloat16)


def with_ends(values, stream_key, least, high):
    spot = [jax.random.randint(jax.random.fold_in(stream_key, axis), (), 0, length) for axis, length in enumerate(values.shape)]
    main_axis = values.shape.index(max(values.shape))
    next_to = spot[:main_axis] + [(spot[main_axis] + 1) % values.shape[main_axis]] + spot[main_axis + 1:]
    return values.at[tuple(spot)].set(least).at[tuple(next_to)].set(high)


def level_of(rng, dims, split, least, high):
    def one(position, shards_of):
        heights = jax.random.uniform(jax.random.fold_in(jax.random.fold_in(rng, 6), position), (shards_of,), jnp.float32, least / len(split), high / len(split))
        return jnp.repeat(jnp.exp(heights), dims[position] // shards_of).reshape((-1,) + (1,) * (len(dims) - position - 1))

    level = one(*split[0])
    for cut in split[1:]:
        level = level * one(*cut)
    return level


def normal_values(key, shape, deviation, reach, pieces=(), dtype=jnp.bfloat16):
    values = deviation * jax.random.normal(key, shape, jnp.float32)
    if pieces:
        values = values * level_of(key, shape, pieces, -0.22, 0.18)
    return jnp.clip(values, -reach, reach).astype(dtype)


def setup_inputs(seed: int = 0) -> dict:
    splits = jax.random.split(jax.random.key(seed), 12)
    query_tokens = draw_query_tokens(jax.random.fold_in(splits[11], 71), 0)
    key_tokens = draw_key_tokens(jax.random.fold_in(splits[11], 71), 0)
    value_tokens = normal_values(splits[2], (IMAGES, SEQ, D), 1.0, 6.0, ((0, 8), (2, 4)))
    head_weight = normal_values(splits[3], (D, EMBED), D ** -0.5, 0.078125, ((0, 4), (1, 8)))
    image_cache = draw_image_cache(jax.random.fold_in(splits[11], 71), 0)
    text_embed = draw_text_embed(jax.random.fold_in(splits[11], 71), 0)
    text_pair = draw_text_pair(jax.random.fold_in(splits[11], 71), 0)
    image_group = with_ends(jax.random.randint(splits[7], (PAIRS,), 0, PAIRS // 2), jax.random.fold_in(splits[7], 1), 0, (PAIRS // 2) - 1).astype(jnp.int32)
    text_group = with_ends(jax.random.randint(splits[8], (PAIRS,), 0, PAIRS // 2), jax.random.fold_in(splits[8], 1), 0, (PAIRS // 2) - 1).astype(jnp.int32)
    logit_scale = jnp.clip(jax.random.uniform(splits[9], (), jnp.float32, 2.6, 2.8), 2.6, 2.8)
    logit_bias = jnp.clip(jax.random.uniform(splits[10], (), jnp.float32, -9.0, -8.0), -9.0, -8.0)
    return dict(query_tokens=query_tokens, key_tokens=key_tokens, value_tokens=value_tokens, head_weight=head_weight, image_cache=image_cache, text_embed=text_embed, text_pair=text_pair, image_group=image_group, text_group=text_group, logit_scale=logit_scale, logit_bias=logit_bias)


loss_scale = 8192.0

def pair_terms(left_rows, right_rows, labels, temper, offset):
    scores = lax.dot_general(left_rows, right_rows, (((1,), (1,)), ((), ())), preferred_element_type=jnp.float32)
    logits = temper * scores + offset
    signed = jnp.where(labels, 1.0, -1.0).astype(jnp.float32)
    margin = signed * logits
    losses = -lax.optimization_barrier(jnp.sum(jax.nn.log_sigmoid(margin), axis=1))
    coeffs = (temper * (-signed * jax.nn.sigmoid(-margin))).astype(jnp.bfloat16)
    return (coeffs, losses)

def head_split(tokens):
    return tokens.reshape(SEQ, HEADS, HEAD_DIM).astype(jnp.float32)

def image_probs(queries, key_heads):
    scores = jnp.einsum('ihd,jhd->hij', queries, key_heads) * (1.0 / math.sqrt(HEAD_DIM))
    return jax.nn.softmax(scores, axis=-1)

def pool_image(tokens):
    query_one, key_one, value_one = tokens
    attn_probs = image_probs(head_split(query_one), head_split(key_one))
    probs_low = lax.optimization_barrier(attn_probs.astype(jnp.bfloat16)).astype(jnp.float32)
    attended = jnp.einsum('hij,jhd->ihd', probs_low, head_split(value_one))
    return lax.optimization_barrier(jnp.mean(attended, axis=0)).reshape(D).astype(jnp.bfloat16)

def grad_image(tokens):
    query_one, key_one, value_one, cotangent = tokens
    queries = head_split(query_one)
    key_heads = head_split(key_one)
    value_heads = head_split(value_one)
    attn_probs = image_probs(queries, key_heads)
    probs_low = lax.optimization_barrier(attn_probs.astype(jnp.bfloat16)).astype(jnp.float32)
    cot_heads = cotangent.reshape(HEADS, HEAD_DIM).astype(jnp.float32)
    prob_grad = jnp.einsum('hd,jhd->hj', cot_heads, value_heads)
    centre = lax.optimization_barrier(jnp.sum(attn_probs * prob_grad[:, None, :], axis=-1, keepdims=True))
    score_grad = (attn_probs * (prob_grad[:, None, :] - centre)).astype(jnp.bfloat16)
    score_grad = lax.optimization_barrier(score_grad).astype(jnp.float32)
    inv_root = 1.0 / math.sqrt(HEAD_DIM)
    query_grad = jnp.einsum('hij,jhd->ihd', score_grad, key_heads) * inv_root
    key_grad = jnp.einsum('hij,ihd->jhd', score_grad, queries) * inv_root
    column_mass = lax.optimization_barrier(jnp.sum(probs_low, axis=1))
    value_grad = jnp.einsum('hj,hd->jhd', column_mass, cot_heads)
    return (query_grad.reshape(SEQ, D).astype(jnp.bfloat16), key_grad.reshape(SEQ, D).astype(jnp.bfloat16), value_grad.reshape(SEQ, D).astype(jnp.bfloat16))

def unit_rows(raw_rows):
    row_norm = lax.rsqrt(lax.optimization_barrier(jnp.sum(raw_rows * raw_rows, axis=1, keepdims=True)) + 1e-06)
    return (raw_rows * row_norm, row_norm)

def reference(query_tokens, key_tokens, value_tokens, head_weight, image_cache, text_embed, text_pair, image_group, text_group, logit_scale, logit_bias):
    pooled = lax.map(pool_image, (query_tokens, key_tokens, value_tokens))
    fresh = jnp.dot(pooled, head_weight, preferred_element_type=jnp.float32)
    fresh_rows = (jnp.arange(IMAGES) * BLOCK).astype(jnp.int32)
    raw_image = image_cache.astype(jnp.float32).at[fresh_rows].set(fresh)
    unit_image, image_norm = unit_rows(raw_image)
    unit_text, text_norm = unit_rows(text_embed.astype(jnp.float32))
    image_low = unit_image.astype(jnp.bfloat16)
    text_low = unit_text.astype(jnp.bfloat16)
    temper = jnp.exp(logit_scale)
    step_rows = min(512, PAIRS)
    blocks = PAIRS // step_rows

    def row_block(text_dir, inputs):
        left_rows, row_index, row_groups = inputs
        labels = (text_pair[None, :] == row_index[:, None]) | (row_groups[:, None] == text_group[None, :])
        coeffs, losses = pair_terms(left_rows, text_low, labels, temper, logit_bias)
        image_dir = jnp.dot(coeffs, text_low, preferred_element_type=jnp.float32)
        text_dir = text_dir + jnp.dot(coeffs.T, left_rows, preferred_element_type=jnp.float32)
        return (text_dir, (image_dir, losses))
    inputs = (image_low.reshape(blocks, step_rows, EMBED), jnp.arange(PAIRS).astype(jnp.int32).reshape(blocks, step_rows), image_group.reshape(blocks, step_rows))
    text_dir, (image_dir, row_loss) = lax.scan(row_block, jnp.zeros((PAIRS, EMBED), jnp.float32), inputs)
    image_dir = image_dir.reshape(PAIRS, EMBED)
    row_loss = row_loss.reshape(PAIRS)
    image_grad = (image_dir - unit_image * lax.optimization_barrier(jnp.sum(unit_image * image_dir, axis=1, keepdims=True))) * image_norm
    text_grad = (text_dir - unit_text * lax.optimization_barrier(jnp.sum(unit_text * text_dir, axis=1, keepdims=True))) * text_norm
    fresh_grad = image_grad[fresh_rows].astype(jnp.bfloat16)
    pooled_grad = jnp.dot(fresh_grad, head_weight.T, preferred_element_type=jnp.float32)
    cotangent = (pooled_grad * (loss_scale / SEQ)).astype(jnp.bfloat16)
    query_grad, key_grad, value_grad = lax.map(grad_image, (query_tokens, key_tokens, value_tokens, cotangent))
    return (query_grad, key_grad, value_grad, image_grad, text_grad, row_loss)
```

```python
import functools
import math

import jax
import jax.numpy as jnp
from jax import lax
from jax.experimental import pallas as pl
from jax.experimental.pallas import tpu as pltpu
from jax.sharding import PartitionSpec as P

HEAD_DIM = 128
LOSS_SCALE = 8192.0
INV_ROOT = 1.0 / math.sqrt(HEAD_DIM)
F32 = jnp.float32
BF16 = jnp.bfloat16
LABEL_BASE = 64
DP_CHUNK = 8


def each_peer(count, body):
    if count <= 8:
        for k in range(1, count):
            body(k)
    else:
        lax.fori_loop(1, count, lambda k, c: (body(k), c)[1], 0)


def probs_t(queries, keys):
    scores = lax.dot_general(keys, queries, (((1,), (1,)), ((), ())), preferred_element_type=F32)
    scores = scores * INV_ROOT
    top = jnp.max(scores, axis=0, keepdims=True)
    grown = jnp.exp(scores - top)
    return grown * (1.0 / jnp.sum(grown, axis=0, keepdims=True))


def forward_kernel(
    n_dp, n_mp, heads, embed,
    q_ref, k_ref, v_ref, w_ref, img_ref, txt_ref, lab_ref, scale_ref, bias_ref,
    p_out, cot_out, igrad_out, tgrad_out, loss_out,
    pairs, probs, pooled, part, cols, fresh, sent, back,
    p_sem, za_s, za_r, xb_s, xb_r, cc_s, cc_r, e2_s, e2_r, e3_s, e3_r, e5_s, e5_r, e4_s, e4_r,
):
    dp = lax.axis_index("dp")
    mp = lax.axis_index("mp")
    n_q = n_dp // 2
    core = lax.rem(dp, 2)
    q_me = dp // 2
    sibling = dp + 1 - 2 * core
    rows = img_ref.shape[0]
    seq = q_ref.shape[1]
    cw = w_ref.shape[1]

    def dp_at(k):
        return lax.rem(dp + k, n_dp)

    def dp_from(k):
        return lax.rem(dp + n_dp - k, n_dp)

    def mp_at(k):
        return lax.rem(mp + k, n_mp)

    def mp_from(k):
        return lax.rem(mp + n_mp - k, n_mp)

    def chip_at(k):
        return 2 * lax.rem(q_me + k, n_q) + core

    def chip_from(k):
        return 2 * lax.rem(q_me + n_q - k, n_q) + core

    barrier = pltpu.get_barrier_semaphore()
    each_peer(n_mp, lambda k: pl.semaphore_signal(
        barrier, inc=1, device_id={"mp": mp_at(k)}, device_id_type=pl.DeviceIdType.MESH))
    each_peer(n_dp, lambda k: pl.semaphore_signal(
        barrier, inc=1, device_id={"dp": dp_at(k)}, device_id_type=pl.DeviceIdType.MESH))

    raw = jnp.concatenate([img_ref[...].astype(F32), txt_ref[...].astype(F32)], axis=0)
    norm = lax.rsqrt(jnp.sum(raw * raw, axis=1, keepdims=True) + 1e-06)
    pairs[dp, mp, :, :embed] = (raw * norm).astype(BF16)
    pairs[dp, mp, :, embed:] = lab_ref[...]
    pl.semaphore_wait(barrier, n_mp - 1 + n_dp - 1)

    def remote(src, dst, s_sem, r_sem, target):
        return pltpu.make_async_remote_copy(
            src_ref=src, dst_ref=dst, send_sem=s_sem, recv_sem=r_sem,
            device_id=target, device_id_type=pl.DeviceIdType.MESH)

    def za(k, slot):
        return remote(pairs.at[dp, slot], pairs.at[dp, slot], za_s.at[k], za_r.at[k], {"mp": mp_at(k)})

    def xb(k, block):
        return remote(pairs.at[block], pairs.at[block], xb_s.at[k], xb_r.at[k], {"dp": chip_at(k)})

    def cc(k, block):
        return remote(pairs.at[block], pairs.at[block], cc_s.at[k], cc_r.at[k], {"dp": sibling})

    each_peer(n_mp, lambda k: za(k, mp).start())

    def head(h):
        at = slice(h * HEAD_DIM, (h + 1) * HEAD_DIM)
        p = probs_t(q_ref[0, :, at], k_ref[0, :, at])
        probs[h] = p
        pltpu.make_async_copy(probs.at[h], p_out.at[h], p_sem.at[h]).start()
        mass = jnp.sum(p.astype(BF16).astype(F32), axis=1, keepdims=True)
        mean = jnp.sum(mass * v_ref[0, :, at].astype(F32), axis=0, keepdims=True) * (1.0 / seq)
        pooled[dp, :, at] = mean.astype(BF16).astype(F32)

    half = heads // 2
    for h in range(half):
        head(h)
    each_peer(n_mp, lambda k: za(k, mp_from(k)).wait_recv())
    each_peer(n_q, lambda k: xb(k, dp).start())
    cc(0, dp).start()
    for h in range(half, heads):
        head(h)

    def e2(k, slot):
        return remote(pooled.at[slot], pooled.at[slot], e2_s.at[k], e2_r.at[k], {"dp": dp_at(k)})

    each_peer(n_dp, lambda k: e2(k, dp).start())

    def relay(k):
        xb(k, chip_from(k)).wait_recv()
        cc(k, chip_from(k)).start()

    each_peer(n_q, relay)
    each_peer(n_dp, lambda k: e2(k, dp_from(k)).wait_recv())
    every = pooled[...].reshape(n_dp, heads * HEAD_DIM).astype(BF16)
    part[mp] = jnp.dot(every, w_ref[...], preferred_element_type=F32)

    def e3(k, slot):
        return remote(part.at[slot], part.at[slot], e3_s.at[k], e3_r.at[k], {"mp": mp_at(k)})

    each_peer(n_mp, lambda k: e3(k, mp).start())
    each_peer(n_mp, lambda k: e3(k, mp_from(k)).wait_recv())
    cols[dp] = jnp.sum(part[...], axis=0)

    def e5(k, slot):
        return remote(cols.at[slot], cols.at[slot], e5_s.at[k], e5_r.at[k], {"dp": dp_at(k)})

    each_peer(n_dp, lambda k: e5(k, dp).start())

    each_peer(n_mp, lambda k: za(k, mp).wait_send())
    each_peer(n_q, lambda k: xb(k, dp).wait_send())

    def settle(k):
        block = 2 * lax.rem(q_me + n_q - k, n_q) + core
        other = 2 * lax.rem(q_me + n_q - k, n_q) + 1 - core
        cc(k, block).wait_send()
        cc(k, other).wait_recv()

    settle(0)
    each_peer(n_q, settle)
    each_peer(n_dp, lambda k: e5(k, dp_from(k)).wait_recv())
    for c in range(n_dp):
        fresh[:, c * cw:(c + 1) * cw] = cols[c]

    raw_fresh = fresh[...]
    fresh_norm = lax.rsqrt(jnp.sum(raw_fresh * raw_fresh, axis=1, keepdims=True) + 1e-06)
    unit_fresh = raw_fresh * fresh_norm
    is_fresh = (lax.broadcasted_iota(jnp.int32, (2 * rows, 1), 0) == 0) & (mp == 0)
    raw = jnp.where(is_fresh, fresh[pl.ds(dp, 1), :], raw)
    norm = lax.rsqrt(jnp.sum(raw * raw, axis=1, keepdims=True) + 1e-06)
    unit = raw * norm

    fresh[...] = unit_fresh
    first = lax.broadcasted_iota(jnp.int32, (2 * rows, 1), 0) == 0

    def put_fresh(b):
        old = pairs[b, 0, :, :embed].astype(F32)
        pairs[b, 0, :, :embed] = jnp.where(first, fresh[pl.ds(b, 1), :], old).astype(BF16)

    put_fresh(0)
    each_peer(n_dp, put_fresh)

    units = jnp.concatenate([unit, unit_fresh], axis=0)
    norms = jnp.concatenate([norm, fresh_norm], axis=0)
    low = units.astype(BF16)
    count = units.shape[0]
    tags = pairs[:, 0, :, embed:].astype(F32)
    lead = lax.broadcasted_iota(jnp.int32, tags.shape, 1) == 0
    fresh_tags = jnp.sum(jnp.where(lead, tags, 0.0), axis=1)
    row_tags = jnp.concatenate([lab_ref[...].astype(F32), fresh_tags], axis=0)
    row_a = row_tags[:, 0:1] * LABEL_BASE + row_tags[:, 1:2]
    row_b = row_tags[:, 2:3] * LABEL_BASE + row_tags[:, 3:4]
    row_spot = lax.broadcasted_iota(jnp.int32, (count, 1), 0)
    row_text = (row_spot >= rows) & (row_spot < 2 * rows)
    temper = jnp.exp(jnp.full((1, 1), scale_ref[0], F32))
    offset = bias_ref[0]

    step = min(DP_CHUNK, n_dp)
    wide = step * n_mp * 2 * rows

    def chunk(at):
        block = pairs[pl.ds(at * step, step), :, :, :embed].reshape(wide, embed)
        col_tags = pairs[pl.ds(at * step, step), :, :, embed:].reshape(wide, 128).astype(F32).T
        col_a = col_tags[0:1, :] * LABEL_BASE + col_tags[1:2, :]
        col_b = col_tags[2:3, :] * LABEL_BASE + col_tags[3:4, :]
        spot = lax.broadcasted_iota(jnp.int32, (1, wide), 1)
        col_text = lax.rem(spot, 2 * rows) >= rows
        valid = row_text != col_text
        scores = lax.dot_general(low, block, (((1,), (1,)), ((), ())), preferred_element_type=F32)
        logits = temper * scores + offset
        signed = jnp.where((row_a == col_a) | (row_b == col_b), 1.0, -1.0)
        margin = signed * logits
        tail = jnp.exp(-jnp.abs(margin))
        log_sig = jnp.minimum(margin, 0.0) - jnp.log1p(tail)
        losses = -jnp.sum(jnp.where(valid, log_sig, 0.0), axis=1, keepdims=True)
        against = jnp.where(margin >= 0, tail, 1.0) / (1.0 + tail)
        coeffs = jnp.where(valid, temper * (-signed * against), 0.0).astype(BF16)
        return jnp.dot(coeffs, block, preferred_element_type=F32), losses

    if n_dp == step:
        direction, losses = chunk(0)
    else:
        def more(at, carry):
            new = chunk(at)
            return carry[0] + new[0], carry[1] + new[1]
        direction, losses = lax.fori_loop(
            0, n_dp // step, more, (jnp.zeros((count, embed), F32), jnp.zeros((count, 1), F32)))

    grads = (direction - units * jnp.sum(units * direction, axis=1, keepdims=True)) * norms
    fresh_low = grads[2 * rows:].astype(BF16)

    if cw % 128 == 0:
        fresh[...] = fresh_low.astype(F32)
        mine = fresh[:, pl.ds(pl.multiple_of(dp * cw, 128), cw)].astype(BF16)
    else:
        spot = lax.broadcasted_iota(jnp.int32, (embed, cw), 0)
        want = lax.broadcasted_iota(jnp.int32, (embed, cw), 1) + dp * cw
        pick = jnp.where(spot == want, 1.0, 0.0).astype(BF16)
        mine = jnp.dot(fresh_low, pick, preferred_element_type=F32).astype(BF16)
    spread = lax.dot_general(mine, w_ref[...], (((1,), (1,)), ((), ())), preferred_element_type=F32)
    for b in range(n_dp):
        sent[b] = spread[b:b + 1, :]
    back[dp] = sent[dp]

    def e4(k, src, dst):
        return remote(sent.at[src], back.at[dst], e4_s.at[k], e4_r.at[k], {"dp": dp_at(k)})

    each_peer(n_dp, lambda k: e4(k, dp_at(k), dp).start())

    igrad_out[...] = grads[:rows]
    tgrad_out[...] = grads[rows:2 * rows]
    loss_out[...] = jnp.broadcast_to(losses[:rows], loss_out.shape)
    for h in range(heads):
        pltpu.make_async_copy(probs.at[h], p_out.at[h], p_sem.at[h]).wait()
    each_peer(n_dp, lambda k: e2(k, dp).wait_send())
    each_peer(n_mp, lambda k: e3(k, mp).wait_send())
    each_peer(n_dp, lambda k: e5(k, dp).wait_send())
    each_peer(n_dp, lambda k: e4(k, dp_at(k), dp_from(k)).wait_recv())
    total = jnp.sum(back[...], axis=0)
    cot_out[...] = (total * (LOSS_SCALE / seq)).astype(BF16).astype(F32)
    each_peer(n_dp, lambda k: e4(k, dp_at(k), dp).wait_send())


def backward_kernel(q_ref, k_ref, v_ref, p_ref, cot_ref, qg_ref, kg_ref, vg_ref):
    p = p_ref[0]
    cot = cot_ref[...]
    prob_grad = jnp.sum(v_ref[0].astype(F32) * cot, axis=1, keepdims=True)
    centre = jnp.sum(p * prob_grad, axis=0, keepdims=True)
    score_grad = (p * (prob_grad - centre)).astype(BF16)
    qg_ref[0] = (lax.dot_general(
        score_grad, k_ref[0], (((0,), (0,)), ((), ())), preferred_element_type=F32
    ) * INV_ROOT).astype(BF16)
    kg_ref[0] = (jnp.dot(score_grad, q_ref[0], preferred_element_type=F32) * INV_ROOT).astype(BF16)
    mass = jnp.sum(p.astype(BF16).astype(F32), axis=1, keepdims=True)
    vg_ref[0] = (mass * cot).astype(BF16)


def on_device(
    n_dp, n_mp,
    query_tokens, key_tokens, value_tokens, head_weight, image_cache, text_embed,
    text_pair, image_group, text_group, logit_scale, logit_bias,
):
    _, seq, width = query_tokens.shape
    heads = width // HEAD_DIM
    rows, embed = image_cache.shape
    cw = head_weight.shape[1]
    dp = lax.axis_index("dp")
    mp = lax.axis_index("mp")
    index = (dp * n_mp + mp) * rows + jnp.arange(rows, dtype=jnp.int32)
    first = jnp.concatenate([index, text_pair])
    second = jnp.concatenate([image_group, text_group])
    lane = jnp.arange(128, dtype=jnp.int32)[None, :]
    first, second = first[:, None], second[:, None]
    labels = jnp.where(
        lane == 0, first // LABEL_BASE,
        jnp.where(lane == 1, first % LABEL_BASE,
                  jnp.where(lane == 2, second // LABEL_BASE, second % LABEL_BASE)),
    ).astype(BF16)

    vmem = pl.BlockSpec(memory_space=pltpu.VMEM)
    smem = pl.BlockSpec(memory_space=pltpu.SMEM)
    n_q = n_dp // 2
    dma = pltpu.SemaphoreType.DMA
    probs, cot, image_grad, text_grad, loss = pl.pallas_call(
        functools.partial(forward_kernel, n_dp, n_mp, heads, embed),
        out_shape=(
            jax.ShapeDtypeStruct((heads, seq, seq), F32),
            jax.ShapeDtypeStruct((1, width), F32),
            jax.ShapeDtypeStruct((rows, embed), F32),
            jax.ShapeDtypeStruct((rows, embed), F32),
            jax.ShapeDtypeStruct((rows, 128), F32),
        ),
        in_specs=[vmem] * 7 + [smem] * 2,
        out_specs=(pl.BlockSpec(memory_space=pl.ANY), vmem, vmem, vmem, vmem),
        scratch_shapes=[
            pltpu.VMEM((n_dp, n_mp, 2 * rows, embed + 128), BF16),
            pltpu.VMEM((heads, seq, seq), F32),
            pltpu.VMEM((n_dp, 1, width), F32),
            pltpu.VMEM((n_mp, n_dp, cw), F32),
            pltpu.VMEM((n_dp, n_dp, cw), F32),
            pltpu.VMEM((n_dp, embed), F32),
            pltpu.VMEM((n_dp, 1, width), F32),
            pltpu.VMEM((n_dp, 1, width), F32),
            dma((heads,)),
            dma((n_mp,)), dma((n_mp,)),
            dma((n_q,)), dma((n_q,)),
            dma((n_q,)), dma((n_q,)),
            dma((n_dp,)), dma((n_dp,)),
            dma((n_mp,)), dma((n_mp,)),
            dma((n_dp,)), dma((n_dp,)),
            dma((n_dp,)), dma((n_dp,)),
        ],
        compiler_params=pltpu.CompilerParams(
            collective_id=0, has_side_effects=True, vmem_limit_bytes=56 * 2**20),
        name="forward_pairs",
    )(
        query_tokens, key_tokens, value_tokens, head_weight, image_cache, text_embed,
        labels, logit_scale.reshape(1), logit_bias.reshape(1),
    )

    token = pl.BlockSpec((1, seq, HEAD_DIM), lambda h: (0, 0, h))
    query_grad, key_grad, value_grad = pl.pallas_call(
        backward_kernel,
        grid=(heads,),
        out_shape=(jax.ShapeDtypeStruct(query_tokens.shape, BF16),) * 3,
        in_specs=[
            token, token, token,
            pl.BlockSpec((1, seq, seq), lambda h: (h, 0, 0)),
            pl.BlockSpec((1, HEAD_DIM), lambda h: (0, h)),
        ],
        out_specs=(token, token, token),
        name="attention_back",
    )(query_tokens, key_tokens, value_tokens, probs, cot)
    return query_grad, key_grad, value_grad, image_grad, text_grad, loss[:, 0]


def solution(mesh):
    pair_rows = P(("dp", "mp"), None)
    pair = P(("dp", "mp"))
    tokens = P("dp", None, "mp")
    return jax.shard_map(
        functools.partial(on_device, mesh.shape["dp"], mesh.shape["mp"]),
        mesh=mesh,
        in_specs=(
            tokens, tokens, tokens, P("mp", "dp"), pair_rows, pair_rows, pair, pair, pair, P(), P(),
        ),
        out_specs=(tokens, tokens, tokens, pair_rows, pair_rows, pair),
        check_vma=False,
    )
```

```python
import functools
import math

import jax
import jax.numpy as jnp
from jax import lax
from jax.experimental import pallas as pl
from jax.experimental.pallas import tpu as pltpu
from jax.sharding import PartitionSpec as P

HEAD_DIM = 128
LOSS_SCALE = 8192.0
INV_ROOT = 1.0 / math.sqrt(HEAD_DIM)
F32 = jnp.float32
BF16 = jnp.bfloat16
LABEL_BASE = 64
LOG2_E = 1.0 / math.log(2.0)
DP_CHUNK = 8


def each_peer(count, body):
    if count <= 8:
        for k in range(1, count):
            body(k)
    else:
        lax.fori_loop(1, count, lambda k, c: (body(k), c)[1], 0)


def probs_t(queries, keys):
    scores = lax.dot_general(keys, queries, (((1,), (1,)), ((), ())), preferred_element_type=F32)
    top = jnp.max(scores, axis=0, keepdims=True)
    grown = jnp.exp2((scores - top) * (INV_ROOT * LOG2_E))
    return grown * (1.0 / jnp.sum(grown, axis=0, keepdims=True))


def column_mass(probs_low):
    ones = jnp.ones((probs_low.shape[1], HEAD_DIM), BF16)
    return jnp.dot(probs_low, ones, preferred_element_type=F32)


def pair_terms(scores, same, valid, temper, offset):
    logits = temper * scores + offset
    signed = jnp.where(same, 1.0, -1.0)
    margin = signed * logits
    tail = jnp.exp(-jnp.abs(margin))
    log_sig = jnp.minimum(margin, 0.0) - jnp.log1p(tail)
    against = jnp.where(margin >= 0, tail, 1.0) / (1.0 + tail)
    coeffs = temper * (-signed * against)
    if valid is not None:
        log_sig = jnp.where(valid, log_sig, 0.0)
        coeffs = jnp.where(valid, coeffs, 0.0)
    return coeffs.astype(BF16), -jnp.sum(log_sig, axis=1, keepdims=True)


def row_labels(tags):
    return tags[:, 0:1] * LABEL_BASE + tags[:, 1:2], tags[:, 2:3] * LABEL_BASE + tags[:, 3:4]


def lane_labels(tags):
    turned = tags.T
    return (turned[0:1, :] * LABEL_BASE + turned[1:2, :],
            turned[2:3, :] * LABEL_BASE + turned[3:4, :])


def nt_dot(left, right):
    return lax.dot_general(left, right, (((1,), (1,)), ((), ())), preferred_element_type=F32)


def forward_kernel(
    n_dp, n_mp, heads, embed,
    q_in, k_in, v_in, w_in, img_ref, txt_ref, tpair_ref, igroup_ref, tgroup_ref, scale_ref, bias_ref,
    p_out, cot_out, igrad_out, tgrad_out, loss_out,
    q_ref, k_ref, v_ref, w_ref, pairs, texts, probs, pooled, part, cols, fresh, sent, back,
    in_sem, p_sem, za_s, za_r, xb_s, xb_r, cc_s, cc_r, e2_s, e2_r, e3_s, e3_r, e5_s, e5_r, e4_s, e4_r,
):
    dp = lax.axis_index("dp")
    mp = lax.axis_index("mp")
    n_q = n_dp // 2
    core = lax.rem(dp, 2)
    q_me = dp // 2
    sibling = dp + 1 - 2 * core
    rows = img_ref.shape[0]
    seq = q_ref.shape[1]
    cw = w_ref.shape[1]

    def dp_at(k):
        return lax.rem(dp + k, n_dp)

    def dp_from(k):
        return lax.rem(dp + n_dp - k, n_dp)

    def mp_at(k):
        return lax.rem(mp + k, n_mp)

    def mp_from(k):
        return lax.rem(mp + n_mp - k, n_mp)

    def chip_at(k):
        return 2 * lax.rem(q_me + k, n_q) + core

    def chip_from(k):
        return 2 * lax.rem(q_me + n_q - k, n_q) + core

    loads = [
        pltpu.make_async_copy(src, dst, in_sem.at[i])
        for i, (src, dst) in enumerate(
            ((q_in, q_ref), (k_in, k_ref), (v_in, v_ref), (w_in, w_ref)))
    ]
    for load in loads:
        load.start()
    barrier = pltpu.get_barrier_semaphore()
    each_peer(n_mp, lambda k: pl.semaphore_signal(
        barrier, inc=1, device_id={"mp": mp_at(k)}, device_id_type=pl.DeviceIdType.MESH))
    each_peer(n_dp, lambda k: pl.semaphore_signal(
        barrier, inc=1, device_id={"dp": dp_at(k)}, device_id_type=pl.DeviceIdType.MESH))

    raw = jnp.concatenate([img_ref[...].astype(F32), txt_ref[...].astype(F32)], axis=0)
    norm = lax.rsqrt(jnp.sum(raw * raw, axis=1, keepdims=True) + 1e-06)
    pairs[dp, mp, :, :embed] = (raw * norm).astype(BF16)
    spot = lax.broadcasted_iota(jnp.int32, (2 * rows, 128), 0)
    lane = lax.broadcasted_iota(jnp.int32, (2 * rows, 128), 1)
    first = (dp * n_mp + mp) * rows + spot
    second = jnp.zeros_like(spot)
    for r in range(rows):
        first = jnp.where(spot == rows + r, tpair_ref[r], first)
        second = jnp.where(spot == r, igroup_ref[r], second)
        second = jnp.where(spot == rows + r, tgroup_ref[r], second)
    label = jnp.where(lane < 2, first, second)
    own_tags = jnp.where(lax.rem(lane, 2) == 0, label // LABEL_BASE, lax.rem(label, LABEL_BASE))
    own_tags = own_tags.astype(F32)
    pairs[dp, mp, :, embed:] = own_tags.astype(BF16)
    pl.semaphore_wait(barrier, n_mp - 1 + n_dp - 1)

    def remote(src, dst, s_sem, r_sem, target):
        return pltpu.make_async_remote_copy(
            src_ref=src, dst_ref=dst, send_sem=s_sem, recv_sem=r_sem,
            device_id=target, device_id_type=pl.DeviceIdType.MESH)

    def za(k, slot):
        return remote(pairs.at[dp, slot], pairs.at[dp, slot], za_s.at[k], za_r.at[k], {"mp": mp_at(k)})

    def xb(k, block):
        return remote(pairs.at[block], pairs.at[block], xb_s.at[k], xb_r.at[k], {"dp": chip_at(k)})

    def cc(k, block):
        return remote(pairs.at[block], pairs.at[block], cc_s.at[k], cc_r.at[k], {"dp": sibling})

    each_peer(n_mp, lambda k: za(k, mp).start())

    for load in loads[:3]:
        load.wait()

    def head(h):
        at = slice(h * HEAD_DIM, (h + 1) * HEAD_DIM)
        p = probs_t(q_ref[0, :, at], k_ref[0, :, at])
        probs[h] = p
        mass = column_mass(p.astype(BF16))
        mean = jnp.sum(mass * v_ref[0, :, at].astype(F32), axis=0, keepdims=True) * (1.0 / seq)
        pooled[dp, :, at] = mean.astype(BF16).astype(F32)

    def keep(h):
        return pltpu.make_async_copy(probs.at[h], p_out.at[h], p_sem.at[h])

    early = 2 * heads // 5
    for h in range(early):
        head(h)
    each_peer(n_mp, lambda k: za(k, mp_from(k)).wait_recv())
    each_peer(n_q, lambda k: xb(k, dp).start())
    cc(0, dp).start()
    for h in range(early, heads):
        head(h)

    def e2(k, slot):
        return remote(pooled.at[slot], pooled.at[slot], e2_s.at[k], e2_r.at[k], {"dp": dp_at(k)})

    each_peer(n_dp, lambda k: e2(k, dp).start())

    for h in range(heads):
        keep(h).start()
    loads[3].wait()
    each_peer(n_dp, lambda k: e2(k, dp_from(k)).wait_recv())
    every = pooled[...].reshape(n_dp, heads * HEAD_DIM).astype(BF16)
    part[mp] = jnp.dot(every, w_ref[...], preferred_element_type=F32)

    def e3(k, slot):
        return remote(part.at[slot], part.at[slot], e3_s.at[k], e3_r.at[k], {"mp": mp_at(k)})

    each_peer(n_mp, lambda k: e3(k, mp).start())

    def relay(k):
        xb(k, chip_from(k)).wait_recv()
        cc(k, chip_from(k)).start()

    each_peer(n_q, relay)
    each_peer(n_mp, lambda k: e3(k, mp_from(k)).wait_recv())
    cols[dp] = jnp.sum(part[...], axis=0)

    def e5(k, slot):
        return remote(cols.at[slot], cols.at[slot], e5_s.at[k], e5_r.at[k], {"dp": dp_at(k)})

    each_peer(n_dp, lambda k: e5(k, dp).start())

    def settle(k):
        block = 2 * lax.rem(q_me + n_q - k, n_q) + 1 - core
        cc(k, block).wait_recv()

    settle(0)
    each_peer(n_q, settle)

    unit = raw * norm
    low = unit.astype(BF16)
    temper = jnp.exp(jnp.full((1, 1), scale_ref[0], F32))
    offset = bias_ref[0]
    own_a, own_b = row_labels(own_tags)
    own_text = lax.broadcasted_iota(jnp.int32, (2 * rows, 1), 0) >= rows
    step = min(DP_CHUNK, n_dp)
    wide = step * n_mp * 2 * rows

    def chunk(at):
        block = pairs[pl.ds(at * step, step), :, :, :embed].reshape(wide, embed)
        col_a, col_b = lane_labels(
            pairs[pl.ds(at * step, step), :, :, embed:].reshape(wide, 128).astype(F32))
        spot = lax.broadcasted_iota(jnp.int32, (1, wide), 1)
        col_text = lax.rem(spot, 2 * rows) >= rows
        valid = (own_text != col_text) & (lax.rem(spot, n_mp * 2 * rows) != 0)
        same = (own_a == col_a) | (own_b == col_b)
        coeffs, losses = pair_terms(nt_dot(low, block), same, valid, temper, offset)
        return jnp.dot(coeffs, block, preferred_element_type=F32), losses

    if n_dp == step:
        direction, losses = chunk(0)
    else:
        def more(at, carry):
            new = chunk(at)
            return carry[0] + new[0], carry[1] + new[1]
        direction, losses = lax.fori_loop(
            0, n_dp // step, more,
            (jnp.zeros((2 * rows, embed), F32), jnp.zeros((2 * rows, 1), F32)))

    def copy_texts(b):
        texts[b] = pairs[b, :, :, :embed].astype(F32)[:, rows:].reshape(
            n_mp * rows, embed).astype(BF16)

    copy_texts(0)
    each_peer(n_dp, copy_texts)
    text_a, text_b = lane_labels(
        pairs[:, :, :, embed:].astype(F32)[:, :, rows:].reshape(n_dp * n_mp * rows, 128))
    tags = pairs[:, 0, :, embed:].astype(F32)
    lead = lax.broadcasted_iota(jnp.int32, tags.shape, 1) == 0
    fresh_tags = jnp.sum(jnp.where(lead, tags, 0.0), axis=1)
    fresh_a, fresh_b = row_labels(fresh_tags)
    fresh_lane_a, fresh_lane_b = lane_labels(fresh_tags)
    fresh_same = (fresh_a == text_a) | (fresh_b == text_b)
    back_same = (own_a[rows:] == fresh_lane_a) | (own_b[rows:] == fresh_lane_b)
    all_texts = texts[...].reshape(n_dp * n_mp * rows, embed)

    each_peer(n_dp, lambda k: e5(k, dp_from(k)).wait_recv())
    for c in range(n_dp):
        fresh[:, c * cw:(c + 1) * cw] = cols[c]
    raw_fresh = fresh[...]
    fresh_norm = lax.rsqrt(jnp.sum(raw_fresh * raw_fresh, axis=1, keepdims=True) + 1e-06)
    unit_fresh = raw_fresh * fresh_norm
    low_fresh = unit_fresh.astype(BF16)
    coeffs, fresh_loss = pair_terms(
        nt_dot(low_fresh, all_texts), fresh_same, None, temper, offset)
    fresh_dir = jnp.dot(coeffs, all_texts, preferred_element_type=F32)
    fresh_grad = (
        fresh_dir - unit_fresh * jnp.sum(unit_fresh * fresh_dir, axis=1, keepdims=True)
    ) * fresh_norm
    fresh_low = fresh_grad.astype(BF16)

    if cw % 128 == 0:
        fresh[...] = fresh_low.astype(F32)
        mine = fresh[:, pl.ds(pl.multiple_of(dp * cw, 128), cw)].astype(BF16)
    else:
        spot = lax.broadcasted_iota(jnp.int32, (embed, cw), 0)
        want = lax.broadcasted_iota(jnp.int32, (embed, cw), 1) + dp * cw
        pick = jnp.where(spot == want, 1.0, 0.0).astype(BF16)
        mine = jnp.dot(fresh_low, pick, preferred_element_type=F32).astype(BF16)
    spread = lax.dot_general(mine, w_ref[...], (((1,), (1,)), ((), ())), preferred_element_type=F32)
    for b in range(n_dp):
        sent[b] = spread[b:b + 1, :]
    back[dp] = sent[dp]

    def e4(k, src, dst):
        return remote(sent.at[src], back.at[dst], e4_s.at[k], e4_r.at[k], {"dp": dp_at(k)})

    each_peer(n_dp, lambda k: e4(k, dp_at(k), dp).start())

    coeffs, unused = pair_terms(
        nt_dot(low[rows:], low_fresh), back_same, None, temper, offset)
    added = jnp.dot(coeffs, low_fresh, preferred_element_type=F32)
    text_dir = direction[rows:] + added
    unit_text = unit[rows:]
    tgrad_out[...] = (
        text_dir - unit_text * jnp.sum(unit_text * text_dir, axis=1, keepdims=True)
    ) * norm[rows:]
    unit_image, image_dir = unit[:rows], direction[:rows]
    image_grad = (
        image_dir - unit_image * jnp.sum(unit_image * image_dir, axis=1, keepdims=True)
    ) * norm[:rows]
    is_fresh = (lax.broadcasted_iota(jnp.int32, (rows, 1), 0) == 0) & (mp == 0)
    fresh[...] = fresh_grad
    igrad_out[...] = jnp.where(is_fresh, fresh[pl.ds(dp, 1), :], image_grad)
    is_mine = lax.broadcasted_iota(jnp.int32, (n_dp, 1), 0) == dp
    my_loss = jnp.sum(jnp.where(is_mine, fresh_loss, 0.0), axis=0, keepdims=True)
    row_loss = jnp.where(is_fresh, my_loss, losses[:rows])
    loss_out[...] = jnp.broadcast_to(row_loss, (rows, 128)).T[0:1, :]

    for h in range(heads):
        keep(h).wait()
    each_peer(n_mp, lambda k: za(k, mp).wait_send())
    each_peer(n_q, lambda k: xb(k, dp).wait_send())
    cc(0, dp).wait_send()
    each_peer(n_q, lambda k: cc(k, chip_from(k)).wait_send())
    each_peer(n_dp, lambda k: e2(k, dp).wait_send())
    each_peer(n_mp, lambda k: e3(k, mp).wait_send())
    each_peer(n_dp, lambda k: e5(k, dp).wait_send())
    each_peer(n_dp, lambda k: e4(k, dp_at(k), dp_from(k)).wait_recv())
    total = jnp.sum(back[...], axis=0)
    cot_out[...] = (total * (LOSS_SCALE / seq)).astype(BF16).astype(F32)
    each_peer(n_dp, lambda k: e4(k, dp_at(k), dp).wait_send())


def backward_kernel(
    group, seq,
    q_ref, k_ref, v_ref, p_ref, cot_ref, igrad_ref, tgrad_ref, loss_ref,
    qg_ref, kg_ref, vg_ref, igrad_out, tgrad_out, loss_out,
):
    @pl.when(pl.program_id(0) == 0)
    def _():
        igrad_out[...] = igrad_ref[...]
        tgrad_out[...] = tgrad_ref[...]
        loss_out[...] = loss_ref[...]

    for h in range(group):
        at = slice(h * HEAD_DIM, (h + 1) * HEAD_DIM)
        p = p_ref[h]
        cot = cot_ref[:, at]
        repeated = jnp.broadcast_to(cot, (HEAD_DIM, HEAD_DIM)).astype(BF16)
        prob_grad = nt_dot(v_ref[0, :, at], repeated)
        prob_grad = jnp.concatenate([prob_grad] * pl.cdiv(seq, HEAD_DIM), axis=1)[:, :seq]
        centre = jnp.sum(p * prob_grad, axis=0, keepdims=True)
        score_grad = (p * (prob_grad - centre)).astype(BF16)
        qg_ref[0, :, at] = (lax.dot_general(
            score_grad, k_ref[0, :, at], (((0,), (0,)), ((), ())), preferred_element_type=F32
        ) * INV_ROOT).astype(BF16)
        kg_ref[0, :, at] = (jnp.dot(
            score_grad, q_ref[0, :, at], preferred_element_type=F32
        ) * INV_ROOT).astype(BF16)
        vg_ref[0, :, at] = (column_mass(p.astype(BF16)) * cot).astype(BF16)


def on_device(
    n_dp, n_mp,
    query_tokens, key_tokens, value_tokens, head_weight, image_cache, text_embed,
    text_pair, image_group, text_group, logit_scale, logit_bias,
):
    _, seq, width = query_tokens.shape
    heads = width // HEAD_DIM
    rows, embed = image_cache.shape
    cw = head_weight.shape[1]
    vmem = pl.BlockSpec(memory_space=pltpu.VMEM)
    any_space = pl.BlockSpec(memory_space=pl.ANY)
    smem = pl.BlockSpec(memory_space=pltpu.SMEM)
    n_q = n_dp // 2
    dma = pltpu.SemaphoreType.DMA
    probs, cot, image_grad, text_grad, loss = pl.pallas_call(
        functools.partial(forward_kernel, n_dp, n_mp, heads, embed),
        out_shape=(
            jax.ShapeDtypeStruct((heads, seq, seq), F32),
            jax.ShapeDtypeStruct((1, width), F32),
            jax.ShapeDtypeStruct((rows, embed), F32),
            jax.ShapeDtypeStruct((rows, embed), F32),
            jax.ShapeDtypeStruct((1, rows), F32),
        ),
        in_specs=[any_space] * 4 + [vmem] * 2 + [smem] * 5,
        out_specs=(any_space, vmem, vmem, vmem, vmem),
        scratch_shapes=[
            pltpu.VMEM(query_tokens.shape, BF16),
            pltpu.VMEM(query_tokens.shape, BF16),
            pltpu.VMEM(query_tokens.shape, BF16),
            pltpu.VMEM(head_weight.shape, BF16),
            pltpu.VMEM((n_dp, n_mp, 2 * rows, embed + 128), BF16),
            pltpu.VMEM((n_dp, n_mp * rows, embed), BF16),
            pltpu.VMEM((heads, seq, seq), F32),
            pltpu.VMEM((n_dp, 1, width), F32),
            pltpu.VMEM((n_mp, n_dp, cw), F32),
            pltpu.VMEM((n_dp, n_dp, cw), F32),
            pltpu.VMEM((n_dp, embed), F32),
            pltpu.VMEM((n_dp, 1, width), F32),
            pltpu.VMEM((n_dp, 1, width), F32),
            dma((4,)),
            dma((heads,)),
            dma((n_mp,)), dma((n_mp,)),
            dma((n_q,)), dma((n_q,)),
            dma((n_q,)), dma((n_q,)),
            dma((n_dp,)), dma((n_dp,)),
            dma((n_mp,)), dma((n_mp,)),
            dma((n_dp,)), dma((n_dp,)),
            dma((n_dp,)), dma((n_dp,)),
        ],
        compiler_params=pltpu.CompilerParams(
            collective_id=0, has_side_effects=True, vmem_limit_bytes=56 * 2**20),
        name="forward_pairs",
    )(
        query_tokens, key_tokens, value_tokens, head_weight, image_cache, text_embed,
        text_pair, image_group, text_group, logit_scale.reshape(1), logit_bias.reshape(1),
    )

    group = 2 if heads % 2 == 0 else 1
    token = pl.BlockSpec((1, seq, group * HEAD_DIM), lambda h: (0, 0, h))
    whole_rows = pl.BlockSpec((rows, embed), lambda h: (0, 0))
    whole_loss = pl.BlockSpec((1, rows), lambda h: (0, 0))
    query_grad, key_grad, value_grad, image_grad, text_grad, loss = pl.pallas_call(
        functools.partial(backward_kernel, group, seq),
        grid=(heads // group,),
        out_shape=(
            jax.ShapeDtypeStruct(query_tokens.shape, BF16),
            jax.ShapeDtypeStruct(query_tokens.shape, BF16),
            jax.ShapeDtypeStruct(query_tokens.shape, BF16),
            jax.ShapeDtypeStruct((rows, embed), F32),
            jax.ShapeDtypeStruct((rows, embed), F32),
            jax.ShapeDtypeStruct((1, rows), F32),
        ),
        in_specs=[
            token, token, token,
            pl.BlockSpec((group, seq, seq), lambda h: (h, 0, 0)),
            pl.BlockSpec((1, group * HEAD_DIM), lambda h: (0, h)),
            whole_rows, whole_rows, whole_loss,
        ],
        out_specs=(token, token, token, whole_rows, whole_rows, whole_loss),
        compiler_params=pltpu.CompilerParams(vmem_limit_bytes=56 * 2**20),
        name="attention_back",
    )(query_tokens, key_tokens, value_tokens, probs, cot, image_grad, text_grad, loss)
    return query_grad, key_grad, value_grad, image_grad, text_grad, loss.reshape(rows)


def solution(mesh):
    pair_rows = P(("dp", "mp"), None)
    pair = P(("dp", "mp"))
    tokens = P("dp", None, "mp")
    return jax.shard_map(
        functools.partial(on_device, mesh.shape["dp"], mesh.shape["mp"]),
        mesh=mesh,
        in_specs=(
            tokens, tokens, tokens, P("mp", "dp"), pair_rows, pair_rows, pair, pair, pair, P(), P(),
        ),
        out_specs=(tokens, tokens, tokens, pair_rows, pair_rows, pair),
        check_vma=False,
    )
```

```python
import functools
import math

import jax
import jax.numpy as jnp
from jax import lax
from jax.experimental import pallas as pl
from jax.experimental.pallas import tpu as pltpu
from jax.sharding import PartitionSpec as P

HEAD_DIM = 128
LOSS_SCALE = 8192.0
INV_ROOT = 1.0 / math.sqrt(HEAD_DIM)
F32 = jnp.float32
BF16 = jnp.bfloat16
LABEL_BASE = 64
HEAD_ROWS = 16
LOG2_E = 1.0 / math.log(2.0)
DP_CHUNK = 8


def each_peer(count, body):
    if count <= 8:
        for k in range(1, count):
            body(k)
    else:
        lax.fori_loop(1, count, lambda k, c: (body(k), c)[1], 0)


def softmax_t(scores):
    top = jnp.max(scores, axis=0, keepdims=True)
    grown = jnp.exp2((scores - top) * (INV_ROOT * LOG2_E))
    return grown * (1.0 / jnp.sum(grown, axis=0, keepdims=True))


def column_mass(probs_low):
    ones = jnp.ones((probs_low.shape[1], HEAD_DIM), BF16)
    return jnp.dot(probs_low, ones, preferred_element_type=F32)


def own_lanes(width):
    shape = (HEAD_ROWS, width)
    head = lax.broadcasted_iota(jnp.int32, shape, 0)
    return lax.broadcasted_iota(jnp.int32, shape, 1) // HEAD_DIM == head


def spread_heads(row):
    wide = jnp.broadcast_to(row.astype(F32), (HEAD_ROWS, row.shape[1]))
    return jnp.where(own_lanes(row.shape[1]), wide, 0.0).astype(BF16)


def sum_heads(left, right):
    full = lax.dot_general(left, right, (((0,), (0,)), ((), ())), preferred_element_type=F32)
    return jnp.sum(jnp.where(own_lanes(right.shape[1]), full, 0.0), axis=0, keepdims=True)


def pair_terms(scores, same, valid, temper, offset):
    logits = temper * scores + offset
    signed = jnp.where(same, 1.0, -1.0)
    margin = signed * logits
    tail = jnp.exp(-jnp.abs(margin))
    log_sig = jnp.minimum(margin, 0.0) - jnp.log1p(tail)
    against = jnp.where(margin >= 0, tail, 1.0) / (1.0 + tail)
    coeffs = temper * (-signed * against)
    if valid is not None:
        log_sig = jnp.where(valid, log_sig, 0.0)
        coeffs = jnp.where(valid, coeffs, 0.0)
    return coeffs.astype(BF16), -jnp.sum(log_sig, axis=1, keepdims=True)


def row_labels(tags):
    return tags[:, 0:1] * LABEL_BASE + tags[:, 1:2], tags[:, 2:3] * LABEL_BASE + tags[:, 3:4]


def lane_labels(tags):
    turned = tags.T
    return (turned[0:1, :] * LABEL_BASE + turned[1:2, :],
            turned[2:3, :] * LABEL_BASE + turned[3:4, :])


def nt_dot(left, right):
    return lax.dot_general(left, right, (((1,), (1,)), ((), ())), preferred_element_type=F32)


def forward_kernel(
    n_dp, n_mp, heads, embed,
    q_in, k_in, v_in, w_in, img_ref, txt_ref, tpair_ref, igroup_ref, tgroup_ref, scale_ref, bias_ref,
    p_out, last_out, cot_out, igrad_out, tgrad_out, loss_out,
    q_ref, k_ref, v_ref, w_ref, pairs, texts, probs, pooled, part, cols, fresh, sent, back,
    in_sem, p_sem, za_s, za_r, xb_s, xb_r, cc_s, cc_r, e2_s, e2_r, e3_s, e3_r, e5_s, e5_r, e4_s, e4_r,
):
    dp = lax.axis_index("dp")
    mp = lax.axis_index("mp")
    n_q = n_dp // 2
    core = lax.rem(dp, 2)
    q_me = dp // 2
    sibling = dp + 1 - 2 * core
    rows = img_ref.shape[0]
    seq = q_ref.shape[1]
    main = seq - 1
    cw = w_ref.shape[1]

    def dp_at(k):
        return lax.rem(dp + k, n_dp)

    def dp_from(k):
        return lax.rem(dp + n_dp - k, n_dp)

    def mp_at(k):
        return lax.rem(mp + k, n_mp)

    def mp_from(k):
        return lax.rem(mp + n_mp - k, n_mp)

    def chip_at(k):
        return 2 * lax.rem(q_me + k, n_q) + core

    def chip_from(k):
        return 2 * lax.rem(q_me + n_q - k, n_q) + core

    loads = [
        pltpu.make_async_copy(src, dst, in_sem.at[i])
        for i, (src, dst) in enumerate(
            ((q_in, q_ref), (k_in, k_ref), (v_in, v_ref), (w_in, w_ref)))
    ]
    for load in loads:
        load.start()
    barrier = pltpu.get_barrier_semaphore()
    each_peer(n_mp, lambda k: pl.semaphore_signal(
        barrier, inc=1, device_id={"mp": mp_at(k)}, device_id_type=pl.DeviceIdType.MESH))
    each_peer(n_dp, lambda k: pl.semaphore_signal(
        barrier, inc=1, device_id={"dp": dp_at(k)}, device_id_type=pl.DeviceIdType.MESH))

    raw = jnp.concatenate([img_ref[...].astype(F32), txt_ref[...].astype(F32)], axis=0)
    norm = lax.rsqrt(jnp.sum(raw * raw, axis=1, keepdims=True) + 1e-06)
    pairs[dp, mp, :, :embed] = (raw * norm).astype(BF16)
    spot = lax.broadcasted_iota(jnp.int32, (2 * rows, 128), 0)
    lane = lax.broadcasted_iota(jnp.int32, (2 * rows, 128), 1)
    first = (dp * n_mp + mp) * rows + spot
    second = jnp.zeros_like(spot)
    for r in range(rows):
        first = jnp.where(spot == rows + r, tpair_ref[r], first)
        second = jnp.where(spot == r, igroup_ref[r], second)
        second = jnp.where(spot == rows + r, tgroup_ref[r], second)
    label = jnp.where(lane < 2, first, second)
    own_tags = jnp.where(lax.rem(lane, 2) == 0, label // LABEL_BASE, lax.rem(label, LABEL_BASE))
    own_tags = own_tags.astype(F32)
    pairs[dp, mp, :, embed:] = own_tags.astype(BF16)
    pl.semaphore_wait(barrier, n_mp - 1 + n_dp - 1)

    def remote(src, dst, s_sem, r_sem, target):
        return pltpu.make_async_remote_copy(
            src_ref=src, dst_ref=dst, send_sem=s_sem, recv_sem=r_sem,
            device_id=target, device_id_type=pl.DeviceIdType.MESH)

    def za(k, slot):
        return remote(pairs.at[dp, slot], pairs.at[dp, slot], za_s.at[k], za_r.at[k], {"mp": mp_at(k)})

    def xb(k, block):
        return remote(pairs.at[block], pairs.at[block], xb_s.at[k], xb_r.at[k], {"dp": chip_at(k)})

    def cc(k, block):
        return remote(pairs.at[block], pairs.at[block], cc_s.at[k], cc_r.at[k], {"dp": sibling})

    each_peer(n_mp, lambda k: za(k, mp).start())

    for load in loads[:3]:
        load.wait()

    last_p = softmax_t(nt_dot(k_ref[0], spread_heads(q_ref[0, main:, :])))
    last_out[...] = last_p
    last_mean = sum_heads(last_p.astype(BF16), v_ref[0])

    def head(h):
        at = slice(h * HEAD_DIM, (h + 1) * HEAD_DIM)
        p = softmax_t(nt_dot(k_ref[0, :, at], q_ref[0, :main, at]))
        probs[h] = p
        mass = column_mass(p.astype(BF16))
        total = jnp.sum(mass * v_ref[0, :, at].astype(F32), axis=0, keepdims=True)
        mean = (total + last_mean[:, at]) * (1.0 / seq)
        pooled[dp, :, at] = mean.astype(BF16).astype(F32)

    def keep(h):
        return pltpu.make_async_copy(probs.at[h], p_out.at[h], p_sem.at[h])

    early = 2 * heads // 5
    for h in range(early):
        head(h)
    each_peer(n_mp, lambda k: za(k, mp_from(k)).wait_recv())
    each_peer(n_q, lambda k: xb(k, dp).start())
    cc(0, dp).start()
    for h in range(early, heads):
        head(h)

    def e2(k, slot):
        return remote(pooled.at[slot], pooled.at[slot], e2_s.at[k], e2_r.at[k], {"dp": dp_at(k)})

    each_peer(n_dp, lambda k: e2(k, dp).start())

    for h in range(heads):
        keep(h).start()
    loads[3].wait()
    each_peer(n_dp, lambda k: e2(k, dp_from(k)).wait_recv())
    every = pooled[...].reshape(n_dp, heads * HEAD_DIM).astype(BF16)
    part[mp] = jnp.dot(every, w_ref[...], preferred_element_type=F32)

    def e3(k, slot):
        return remote(part.at[slot], part.at[slot], e3_s.at[k], e3_r.at[k], {"mp": mp_at(k)})

    each_peer(n_mp, lambda k: e3(k, mp).start())

    def relay(k):
        xb(k, chip_from(k)).wait_recv()
        cc(k, chip_from(k)).start()

    each_peer(n_q, relay)
    each_peer(n_mp, lambda k: e3(k, mp_from(k)).wait_recv())
    cols[dp] = jnp.sum(part[...], axis=0)

    def e5(k, slot):
        return remote(cols.at[slot], cols.at[slot], e5_s.at[k], e5_r.at[k], {"dp": dp_at(k)})

    each_peer(n_dp, lambda k: e5(k, dp).start())

    def settle(k):
        block = 2 * lax.rem(q_me + n_q - k, n_q) + 1 - core
        cc(k, block).wait_recv()

    settle(0)
    each_peer(n_q, settle)

    unit = raw * norm
    low = unit.astype(BF16)
    temper = jnp.exp(jnp.full((1, 1), scale_ref[0], F32))
    offset = bias_ref[0]
    own_a, own_b = row_labels(own_tags)
    own_text = lax.broadcasted_iota(jnp.int32, (2 * rows, 1), 0) >= rows
    step = min(DP_CHUNK, n_dp)
    wide = step * n_mp * 2 * rows

    def chunk(at):
        block = pairs[pl.ds(at * step, step), :, :, :embed].reshape(wide, embed)
        col_a, col_b = lane_labels(
            pairs[pl.ds(at * step, step), :, :, embed:].reshape(wide, 128).astype(F32))
        spot = lax.broadcasted_iota(jnp.int32, (1, wide), 1)
        col_text = lax.rem(spot, 2 * rows) >= rows
        valid = (own_text != col_text) & (lax.rem(spot, n_mp * 2 * rows) != 0)
        same = (own_a == col_a) | (own_b == col_b)
        coeffs, losses = pair_terms(nt_dot(low, block), same, valid, temper, offset)
        return jnp.dot(coeffs, block, preferred_element_type=F32), losses

    if n_dp == step:
        direction, losses = chunk(0)
    else:
        def more(at, carry):
            new = chunk(at)
            return carry[0] + new[0], carry[1] + new[1]
        direction, losses = lax.fori_loop(
            0, n_dp // step, more,
            (jnp.zeros((2 * rows, embed), F32), jnp.zeros((2 * rows, 1), F32)))

    def copy_texts(b):
        texts[b] = pairs[b, :, :, :embed].astype(F32)[:, rows:].reshape(
            n_mp * rows, embed).astype(BF16)

    copy_texts(0)
    each_peer(n_dp, copy_texts)
    text_a, text_b = lane_labels(
        pairs[:, :, :, embed:].astype(F32)[:, :, rows:].reshape(n_dp * n_mp * rows, 128))
    tags = pairs[:, 0, :, embed:].astype(F32)
    lead = lax.broadcasted_iota(jnp.int32, tags.shape, 1) == 0
    fresh_tags = jnp.sum(jnp.where(lead, tags, 0.0), axis=1)
    fresh_a, fresh_b = row_labels(fresh_tags)
    fresh_lane_a, fresh_lane_b = lane_labels(fresh_tags)
    fresh_same = (fresh_a == text_a) | (fresh_b == text_b)
    back_same = (own_a[rows:] == fresh_lane_a) | (own_b[rows:] == fresh_lane_b)
    all_texts = texts[...].reshape(n_dp * n_mp * rows, embed)

    each_peer(n_dp, lambda k: e5(k, dp_from(k)).wait_recv())
    for c in range(n_dp):
        fresh[:, c * cw:(c + 1) * cw] = cols[c]
    raw_fresh = fresh[...]
    fresh_norm = lax.rsqrt(jnp.sum(raw_fresh * raw_fresh, axis=1, keepdims=True) + 1e-06)
    unit_fresh = raw_fresh * fresh_norm
    low_fresh = unit_fresh.astype(BF16)
    coeffs, fresh_loss = pair_terms(
        nt_dot(low_fresh, all_texts), fresh_same, None, temper, offset)
    fresh_dir = jnp.dot(coeffs, all_texts, preferred_element_type=F32)
    fresh_grad = (
        fresh_dir - unit_fresh * jnp.sum(unit_fresh * fresh_dir, axis=1, keepdims=True)
    ) * fresh_norm
    fresh_low = fresh_grad.astype(BF16)

    if cw % 128 == 0:
        fresh[...] = fresh_low.astype(F32)
        mine = fresh[:, pl.ds(pl.multiple_of(dp * cw, 128), cw)].astype(BF16)
    else:
        spot = lax.broadcasted_iota(jnp.int32, (embed, cw), 0)
        want = lax.broadcasted_iota(jnp.int32, (embed, cw), 1) + dp * cw
        pick = jnp.where(spot == want, 1.0, 0.0).astype(BF16)
        mine = jnp.dot(fresh_low, pick, preferred_element_type=F32).astype(BF16)
    spread = lax.dot_general(mine, w_ref[...], (((1,), (1,)), ((), ())), preferred_element_type=F32)
    for b in range(n_dp):
        sent[b] = spread[b:b + 1, :]
    back[dp] = sent[dp]

    def e4(k, src, dst):
        return remote(sent.at[src], back.at[dst], e4_s.at[k], e4_r.at[k], {"dp": dp_at(k)})

    each_peer(n_dp, lambda k: e4(k, dp_at(k), dp).start())

    coeffs, unused = pair_terms(
        nt_dot(low[rows:], low_fresh), back_same, None, temper, offset)
    added = jnp.dot(coeffs, low_fresh, preferred_element_type=F32)
    text_dir = direction[rows:] + added
    unit_text = unit[rows:]
    tgrad_out[...] = (
        text_dir - unit_text * jnp.sum(unit_text * text_dir, axis=1, keepdims=True)
    ) * norm[rows:]
    unit_image, image_dir = unit[:rows], direction[:rows]
    image_grad = (
        image_dir - unit_image * jnp.sum(unit_image * image_dir, axis=1, keepdims=True)
    ) * norm[:rows]
    is_fresh = (lax.broadcasted_iota(jnp.int32, (rows, 1), 0) == 0) & (mp == 0)
    fresh[...] = fresh_grad
    igrad_out[...] = jnp.where(is_fresh, fresh[pl.ds(dp, 1), :], image_grad)
    is_mine = lax.broadcasted_iota(jnp.int32, (n_dp, 1), 0) == dp
    my_loss = jnp.sum(jnp.where(is_mine, fresh_loss, 0.0), axis=0, keepdims=True)
    row_loss = jnp.where(is_fresh, my_loss, losses[:rows])
    loss_out[...] = jnp.broadcast_to(row_loss, (rows, 128)).T[0:1, :]

    for h in range(heads):
        keep(h).wait()
    each_peer(n_mp, lambda k: za(k, mp).wait_send())
    each_peer(n_q, lambda k: xb(k, dp).wait_send())
    cc(0, dp).wait_send()
    each_peer(n_q, lambda k: cc(k, chip_from(k)).wait_send())
    each_peer(n_dp, lambda k: e2(k, dp).wait_send())
    each_peer(n_mp, lambda k: e3(k, mp).wait_send())
    each_peer(n_dp, lambda k: e5(k, dp).wait_send())
    each_peer(n_dp, lambda k: e4(k, dp_at(k), dp_from(k)).wait_recv())
    total = jnp.sum(back[...], axis=0)
    cot_out[...] = (total * (LOSS_SCALE / seq)).astype(BF16).astype(F32)
    each_peer(n_dp, lambda k: e4(k, dp_at(k), dp).wait_send())


def backward_kernel(
    heads, group,
    q_in, k_in, v_in, p_in, last_ref, cot_ref, igrad_ref, tgrad_ref, loss_ref,
    qg_out, kg_out, vg_out, igrad_out, tgrad_out, loss_out,
    q_ref, k_ref, v_ref, p_ref, qg_ref, kg_ref, vg_ref, in_sem, p_sem, out_sem,
):
    seq, width = q_ref.shape[1:]
    main = seq - 1

    def load_probs(h):
        return pltpu.make_async_copy(p_in.at[h], p_ref.at[h], p_sem.at[h])

    loads = [
        pltpu.make_async_copy(src, dst, in_sem.at[i])
        for i, (src, dst) in enumerate(((v_in, v_ref), (k_in, k_ref), (q_in, q_ref)))
    ]
    for load in loads:
        load.start()
    for h in range(heads):
        load_probs(h).start()
    igrad_out[...] = igrad_ref[...]
    tgrad_out[...] = tgrad_ref[...]
    loss_out[...] = loss_ref[...]
    for load in loads:
        load.wait()

    def store(part, i):
        ref, out = ((qg_ref, qg_out), (kg_ref, kg_out), (vg_ref, vg_out))[i]
        at = pl.ds(part * group * HEAD_DIM, group * HEAD_DIM)
        return pltpu.make_async_copy(ref.at[:, :, at], out.at[:, :, at], out_sem.at[i, part])

    last_p = last_ref[...]
    last_low = last_p.astype(BF16)
    last_grad = nt_dot(v_ref[0], spread_heads(cot_ref[...]))
    centre = jnp.sum(last_p * last_grad, axis=0, keepdims=True)
    last_score = (last_p * (last_grad - centre)).astype(BF16)
    last_query = spread_heads(q_ref[0, main:, :])
    qg_ref[0, main:, :] = (sum_heads(last_score, k_ref[0]) * INV_ROOT).astype(BF16)
    head_row = lax.broadcasted_iota(jnp.int32, (HEAD_ROWS, HEAD_DIM), 0)

    for h in range(heads):
        at = slice(h * HEAD_DIM, (h + 1) * HEAD_DIM)
        load_probs(h).wait()
        p = p_ref[h]
        cot = cot_ref[:, at]
        repeated = jnp.broadcast_to(cot, (HEAD_DIM, HEAD_DIM)).astype(BF16)
        prob_grad = nt_dot(v_ref[0, :, at], repeated)
        prob_grad = jnp.concatenate([prob_grad] * (main // HEAD_DIM), axis=1)
        centre = jnp.sum(p * prob_grad, axis=0, keepdims=True)
        score_grad = (p * (prob_grad - centre)).astype(BF16)
        qg_ref[0, :main, at] = (lax.dot_general(
            score_grad, k_ref[0, :, at], (((0,), (0,)), ((), ())), preferred_element_type=F32
        ) * INV_ROOT).astype(BF16)
        kg_ref[0, :, at] = ((
            jnp.dot(score_grad, q_ref[0, :main, at], preferred_element_type=F32)
            + jnp.dot(last_score, last_query[:, at], preferred_element_type=F32)
        ) * INV_ROOT).astype(BF16)
        pick = jnp.where(head_row == h, 1.0, 0.0).astype(BF16)
        mass = column_mass(p.astype(BF16)) + jnp.dot(
            last_low, pick, preferred_element_type=F32)
        vg_ref[0, :, at] = (mass * cot).astype(BF16)
        if (h + 1) % group == 0:
            for i in range(3):
                store(h // group, i).start()
    for part in range(heads // group):
        for i in range(3):
            store(part, i).wait()


def on_device(
    n_dp, n_mp,
    query_tokens, key_tokens, value_tokens, head_weight, image_cache, text_embed,
    text_pair, image_group, text_group, logit_scale, logit_bias,
):
    _, seq, width = query_tokens.shape
    heads = width // HEAD_DIM
    rows, embed = image_cache.shape
    cw = head_weight.shape[1]
    vmem = pl.BlockSpec(memory_space=pltpu.VMEM)
    any_space = pl.BlockSpec(memory_space=pl.ANY)
    smem = pl.BlockSpec(memory_space=pltpu.SMEM)
    n_q = n_dp // 2
    dma = pltpu.SemaphoreType.DMA
    probs, last_probs, cot, image_grad, text_grad, loss = pl.pallas_call(
        functools.partial(forward_kernel, n_dp, n_mp, heads, embed),
        out_shape=(
            jax.ShapeDtypeStruct((heads, seq, seq - 1), F32),
            jax.ShapeDtypeStruct((seq, HEAD_ROWS), F32),
            jax.ShapeDtypeStruct((1, width), F32),
            jax.ShapeDtypeStruct((rows, embed), F32),
            jax.ShapeDtypeStruct((rows, embed), F32),
            jax.ShapeDtypeStruct((1, rows), F32),
        ),
        in_specs=[any_space] * 4 + [vmem] * 2 + [smem] * 5,
        out_specs=(any_space, vmem, vmem, vmem, vmem, vmem),
        scratch_shapes=[
            pltpu.VMEM(query_tokens.shape, BF16),
            pltpu.VMEM(query_tokens.shape, BF16),
            pltpu.VMEM(query_tokens.shape, BF16),
            pltpu.VMEM(head_weight.shape, BF16),
            pltpu.VMEM((n_dp, n_mp, 2 * rows, embed + 128), BF16),
            pltpu.VMEM((n_dp, n_mp * rows, embed), BF16),
            pltpu.VMEM((heads, seq, seq - 1), F32),
            pltpu.VMEM((n_dp, 1, width), F32),
            pltpu.VMEM((n_mp, n_dp, cw), F32),
            pltpu.VMEM((n_dp, n_dp, cw), F32),
            pltpu.VMEM((n_dp, embed), F32),
            pltpu.VMEM((n_dp, 1, width), F32),
            pltpu.VMEM((n_dp, 1, width), F32),
            dma((4,)),
            dma((heads,)),
            dma((n_mp,)), dma((n_mp,)),
            dma((n_q,)), dma((n_q,)),
            dma((n_q,)), dma((n_q,)),
            dma((n_dp,)), dma((n_dp,)),
            dma((n_mp,)), dma((n_mp,)),
            dma((n_dp,)), dma((n_dp,)),
            dma((n_dp,)), dma((n_dp,)),
        ],
        compiler_params=pltpu.CompilerParams(
            collective_id=0, has_side_effects=True, vmem_limit_bytes=56 * 2**20),
        name="forward_pairs",
    )(
        query_tokens, key_tokens, value_tokens, head_weight, image_cache, text_embed,
        text_pair, image_group, text_group, logit_scale.reshape(1), logit_bias.reshape(1),
    )

    group = 2 if heads % 2 == 0 else 1
    query_grad, key_grad, value_grad, image_grad, text_grad, loss = pl.pallas_call(
        functools.partial(backward_kernel, heads, group),
        out_shape=(
            jax.ShapeDtypeStruct(query_tokens.shape, BF16),
            jax.ShapeDtypeStruct(query_tokens.shape, BF16),
            jax.ShapeDtypeStruct(query_tokens.shape, BF16),
            jax.ShapeDtypeStruct((rows, embed), F32),
            jax.ShapeDtypeStruct((rows, embed), F32),
            jax.ShapeDtypeStruct((1, rows), F32),
        ),
        in_specs=[any_space] * 4 + [vmem] * 5,
        out_specs=(any_space,) * 3 + (vmem,) * 3,
        scratch_shapes=[
            pltpu.VMEM(query_tokens.shape, BF16),
            pltpu.VMEM(query_tokens.shape, BF16),
            pltpu.VMEM(query_tokens.shape, BF16),
            pltpu.VMEM((heads, seq, seq - 1), F32),
            pltpu.VMEM(query_tokens.shape, BF16),
            pltpu.VMEM(query_tokens.shape, BF16),
            pltpu.VMEM(query_tokens.shape, BF16),
            dma((3,)), dma((heads,)), dma((3, heads // group)),
        ],
        compiler_params=pltpu.CompilerParams(vmem_limit_bytes=56 * 2**20),
        name="attention_back",
    )(query_tokens, key_tokens, value_tokens, probs, last_probs, cot, image_grad, text_grad, loss)
    return query_grad, key_grad, value_grad, image_grad, text_grad, loss.reshape(rows)


def solution(mesh):
    pair_rows = P(("dp", "mp"), None)
    pair = P(("dp", "mp"))
    tokens = P("dp", None, "mp")
    return jax.shard_map(
        functools.partial(on_device, mesh.shape["dp"], mesh.shape["mp"]),
        mesh=mesh,
        in_specs=(
            tokens, tokens, tokens, P("mp", "dp"), pair_rows, pair_rows, pair, pair, pair, P(), P(),
        ),
        out_specs=(tokens, tokens, tokens, pair_rows, pair_rows, pair),
        check_vma=False,
    )
```

```python
import functools
import math

import jax
import jax.numpy as jnp
from jax import lax
from jax.experimental import pallas as pl
from jax.experimental.pallas import tpu as pltpu
from jax.sharding import PartitionSpec as P

HEAD_DIM = 128
LOSS_SCALE = 8192.0
INV_ROOT = 1.0 / math.sqrt(HEAD_DIM)
F32 = jnp.float32
BF16 = jnp.bfloat16
LABEL_BASE = 64
HEAD_ROWS = 16
LOG2_E = 1.0 / math.log(2.0)
DP_CHUNK = 8


def each_peer(count, body):
    if count <= 8:
        for k in range(1, count):
            body(k)
    else:
        lax.fori_loop(1, count, lambda k, c: (body(k), c)[1], 0)


def softmax_t(scores):
    top = jnp.max(scores, axis=0, keepdims=True)
    grown = jnp.exp2((scores - top) * (INV_ROOT * LOG2_E))
    return grown * (1.0 / jnp.sum(grown, axis=0, keepdims=True))


def column_mass(probs_low):
    ones = jnp.ones((probs_low.shape[1], HEAD_DIM), BF16)
    return jnp.dot(probs_low, ones, preferred_element_type=F32)


def own_lanes(width, start=0):
    shape = (HEAD_ROWS, width)
    head = lax.broadcasted_iota(jnp.int32, shape, 0)
    return lax.broadcasted_iota(jnp.int32, shape, 1) // HEAD_DIM + start == head


def spread_heads(row, start=0):
    wide = jnp.broadcast_to(row.astype(F32), (HEAD_ROWS, row.shape[1]))
    return jnp.where(own_lanes(row.shape[1], start), wide, 0.0).astype(BF16)


def sum_heads(left, right, start=0):
    full = lax.dot_general(left, right, (((0,), (0,)), ((), ())), preferred_element_type=F32)
    own = own_lanes(right.shape[1], start)
    return jnp.sum(jnp.where(own, full, 0.0), axis=0, keepdims=True)


def pair_terms(scores, same, valid, temper, offset):
    logits = temper * scores + offset
    signed = jnp.where(same, 1.0, -1.0)
    margin = signed * logits
    tail = jnp.exp(-jnp.abs(margin))
    log_sig = jnp.minimum(margin, 0.0) - jnp.log1p(tail)
    against = jnp.where(margin >= 0, tail, 1.0) / (1.0 + tail)
    coeffs = temper * (-signed * against)
    if valid is not None:
        log_sig = jnp.where(valid, log_sig, 0.0)
        coeffs = jnp.where(valid, coeffs, 0.0)
    return coeffs.astype(BF16), -jnp.sum(log_sig, axis=1, keepdims=True)


def row_labels(tags):
    return tags[:, 0:1] * LABEL_BASE + tags[:, 1:2], tags[:, 2:3] * LABEL_BASE + tags[:, 3:4]


def lane_labels(tags):
    turned = tags.T
    return (turned[0:1, :] * LABEL_BASE + turned[1:2, :],
            turned[2:3, :] * LABEL_BASE + turned[3:4, :])


def nt_dot(left, right):
    return lax.dot_general(left, right, (((1,), (1,)), ((), ())), preferred_element_type=F32)


def forward_kernel(
    n_dp, n_mp, heads, embed,
    q_in, k_in, v_in, w_in, img_ref, txt_ref, tpair_ref, igroup_ref, tgroup_ref, scale_ref, bias_ref,
    p_out, last_out, cot_out, igrad_out, tgrad_out, loss_out,
    q_ref, k_ref, v_ref, w_ref, pairs, texts, probs, pooled, part, cols, fresh, sent, back,
    in_sem, p_sem, za_s, za_r, xb_s, xb_r, cc_s, cc_r, e2_s, e2_r, e3_s, e3_r, e5_s, e5_r, e4_s, e4_r,
):
    dp = lax.axis_index("dp")
    mp = lax.axis_index("mp")
    n_q = n_dp // 2
    core = lax.rem(dp, 2)
    q_me = dp // 2
    sibling = dp + 1 - 2 * core
    rows = img_ref.shape[0]
    seq = q_ref.shape[1]
    main = seq - 1
    cw = w_ref.shape[1]

    def dp_at(k):
        return lax.rem(dp + k, n_dp)

    def dp_from(k):
        return lax.rem(dp + n_dp - k, n_dp)

    def mp_at(k):
        return lax.rem(mp + k, n_mp)

    def mp_from(k):
        return lax.rem(mp + n_mp - k, n_mp)

    def chip_at(k):
        return 2 * lax.rem(q_me + k, n_q) + core

    def chip_from(k):
        return 2 * lax.rem(q_me + n_q - k, n_q) + core

    loads = [
        pltpu.make_async_copy(src, dst, in_sem.at[i])
        for i, (src, dst) in enumerate(
            ((q_in, q_ref), (k_in, k_ref), (v_in, v_ref), (w_in, w_ref)))
    ]
    for load in loads:
        load.start()
    barrier = pltpu.get_barrier_semaphore()
    each_peer(n_mp, lambda k: pl.semaphore_signal(
        barrier, inc=1, device_id={"mp": mp_at(k)}, device_id_type=pl.DeviceIdType.MESH))
    each_peer(n_dp, lambda k: pl.semaphore_signal(
        barrier, inc=1, device_id={"dp": dp_at(k)}, device_id_type=pl.DeviceIdType.MESH))

    raw = jnp.concatenate([img_ref[...].astype(F32), txt_ref[...].astype(F32)], axis=0)
    norm = lax.rsqrt(jnp.sum(raw * raw, axis=1, keepdims=True) + 1e-06)
    pairs[dp, mp, :, :embed] = (raw * norm).astype(BF16)
    spot = lax.broadcasted_iota(jnp.int32, (2 * rows, 128), 0)
    lane = lax.broadcasted_iota(jnp.int32, (2 * rows, 128), 1)
    first = (dp * n_mp + mp) * rows + spot
    second = jnp.zeros_like(spot)
    for r in range(rows):
        first = jnp.where(spot == rows + r, tpair_ref[r], first)
        second = jnp.where(spot == r, igroup_ref[r], second)
        second = jnp.where(spot == rows + r, tgroup_ref[r], second)
    label = jnp.where(lane < 2, first, second)
    own_tags = jnp.where(lax.rem(lane, 2) == 0, label // LABEL_BASE, lax.rem(label, LABEL_BASE))
    own_tags = own_tags.astype(F32)
    pairs[dp, mp, :, embed:] = own_tags.astype(BF16)
    pl.semaphore_wait(barrier, n_mp - 1 + n_dp - 1)

    def remote(src, dst, s_sem, r_sem, target):
        return pltpu.make_async_remote_copy(
            src_ref=src, dst_ref=dst, send_sem=s_sem, recv_sem=r_sem,
            device_id=target, device_id_type=pl.DeviceIdType.MESH)

    def za(k, slot):
        return remote(pairs.at[dp, slot], pairs.at[dp, slot], za_s.at[k], za_r.at[k], {"mp": mp_at(k)})

    def xb(k, block):
        return remote(pairs.at[block], pairs.at[block], xb_s.at[k], xb_r.at[k], {"dp": chip_at(k)})

    def cc(k, block):
        return remote(pairs.at[block], pairs.at[block], cc_s.at[k], cc_r.at[k], {"dp": sibling})

    each_peer(n_mp, lambda k: za(k, mp).start())

    for load in loads[:3]:
        load.wait()

    last_p = softmax_t(nt_dot(k_ref[0], spread_heads(q_ref[0, main:, :])))
    last_out[...] = last_p
    last_mean = sum_heads(last_p.astype(BF16), v_ref[0])

    def head(h):
        at = pl.ds(pl.multiple_of(h * HEAD_DIM, HEAD_DIM), HEAD_DIM)
        p = softmax_t(nt_dot(k_ref[0, :, at], q_ref[0, :main, at]))
        probs[h] = p
        mass = column_mass(p.astype(BF16))
        pooled[dp, :, at] = jnp.sum(mass * v_ref[0, :, at].astype(F32), axis=0, keepdims=True)

    def keep(h):
        return pltpu.make_async_copy(probs.at[h], p_out.at[h], p_sem.at[h])

    group = 2 if heads % 2 == 0 else 1

    def some_heads(i, carry):
        for u in range(group):
            head(i * group + u)

        @pl.when(i == 1)
        def _():
            each_peer(n_mp, lambda k: za(k, mp_from(k)).wait_recv())
            each_peer(n_q, lambda k: xb(k, dp).start())
            cc(0, dp).start()

        return carry

    lax.fori_loop(0, heads // group, some_heads, 0)
    mean = (pooled[dp] + last_mean) * (1.0 / seq)
    pooled[dp] = mean.astype(BF16).astype(F32)

    def e2(k, slot):
        return remote(pooled.at[slot], pooled.at[slot], e2_s.at[k], e2_r.at[k], {"dp": dp_at(k)})

    each_peer(n_dp, lambda k: e2(k, dp).start())

    for h in range(heads):
        keep(h).start()
    loads[3].wait()
    each_peer(n_dp, lambda k: e2(k, dp_from(k)).wait_recv())
    every = pooled[...].reshape(n_dp, heads * HEAD_DIM).astype(BF16)
    part[mp] = jnp.dot(every, w_ref[...], preferred_element_type=F32)

    def e3(k, slot):
        return remote(part.at[slot], part.at[slot], e3_s.at[k], e3_r.at[k], {"mp": mp_at(k)})

    each_peer(n_mp, lambda k: e3(k, mp).start())

    def relay(k):
        xb(k, chip_from(k)).wait_recv()
        cc(k, chip_from(k)).start()

    each_peer(n_q, relay)
    each_peer(n_mp, lambda k: e3(k, mp_from(k)).wait_recv())
    cols[dp] = jnp.sum(part[...], axis=0)

    def e5(k, slot):
        return remote(cols.at[slot], cols.at[slot], e5_s.at[k], e5_r.at[k], {"dp": dp_at(k)})

    each_peer(n_dp, lambda k: e5(k, dp).start())

    def settle(k):
        block = 2 * lax.rem(q_me + n_q - k, n_q) + 1 - core
        cc(k, block).wait_recv()

    settle(0)
    each_peer(n_q, settle)

    unit = raw * norm
    low = unit.astype(BF16)
    temper = jnp.exp(jnp.full((1, 1), scale_ref[0], F32))
    offset = bias_ref[0]
    own_a, own_b = row_labels(own_tags)
    own_text = lax.broadcasted_iota(jnp.int32, (2 * rows, 1), 0) >= rows
    step = min(DP_CHUNK, n_dp)
    wide = step * n_mp * 2 * rows

    def chunk(at):
        block = pairs[pl.ds(at * step, step), :, :, :embed].reshape(wide, embed)
        col_a, col_b = lane_labels(
            pairs[pl.ds(at * step, step), :, :, embed:].reshape(wide, 128).astype(F32))
        spot = lax.broadcasted_iota(jnp.int32, (1, wide), 1)
        col_text = lax.rem(spot, 2 * rows) >= rows
        valid = (own_text != col_text) & (lax.rem(spot, n_mp * 2 * rows) != 0)
        same = (own_a == col_a) | (own_b == col_b)
        coeffs, losses = pair_terms(nt_dot(low, block), same, valid, temper, offset)
        return jnp.dot(coeffs, block, preferred_element_type=F32), losses

    if n_dp == step:
        direction, losses = chunk(0)
    else:
        def more(at, carry):
            new = chunk(at)
            return carry[0] + new[0], carry[1] + new[1]
        direction, losses = lax.fori_loop(
            0, n_dp // step, more,
            (jnp.zeros((2 * rows, embed), F32), jnp.zeros((2 * rows, 1), F32)))

    def copy_texts(b):
        texts[b] = pairs[b, :, :, :embed].astype(F32)[:, rows:].reshape(
            n_mp * rows, embed).astype(BF16)

    copy_texts(0)
    each_peer(n_dp, copy_texts)
    text_a, text_b = lane_labels(
        pairs[:, :, :, embed:].astype(F32)[:, :, rows:].reshape(n_dp * n_mp * rows, 128))
    tags = pairs[:, 0, :, embed:].astype(F32)
    lead = lax.broadcasted_iota(jnp.int32, tags.shape, 1) == 0
    fresh_tags = jnp.sum(jnp.where(lead, tags, 0.0), axis=1)
    fresh_a, fresh_b = row_labels(fresh_tags)
    fresh_lane_a, fresh_lane_b = lane_labels(fresh_tags)
    fresh_same = (fresh_a == text_a) | (fresh_b == text_b)
    back_same = (own_a[rows:] == fresh_lane_a) | (own_b[rows:] == fresh_lane_b)
    all_texts = texts[...].reshape(n_dp * n_mp * rows, embed)

    each_peer(n_dp, lambda k: e5(k, dp_from(k)).wait_recv())
    for c in range(n_dp):
        fresh[:, c * cw:(c + 1) * cw] = cols[c]
    raw_fresh = fresh[...]
    fresh_norm = lax.rsqrt(jnp.sum(raw_fresh * raw_fresh, axis=1, keepdims=True) + 1e-06)
    unit_fresh = raw_fresh * fresh_norm
    low_fresh = unit_fresh.astype(BF16)
    coeffs, fresh_loss = pair_terms(
        nt_dot(low_fresh, all_texts), fresh_same, None, temper, offset)
    fresh_dir = jnp.dot(coeffs, all_texts, preferred_element_type=F32)
    fresh_grad = (
        fresh_dir - unit_fresh * jnp.sum(unit_fresh * fresh_dir, axis=1, keepdims=True)
    ) * fresh_norm
    fresh_low = fresh_grad.astype(BF16)

    if cw % 128 == 0:
        fresh[...] = fresh_low.astype(F32)
        mine = fresh[:, pl.ds(pl.multiple_of(dp * cw, 128), cw)].astype(BF16)
    else:
        spot = lax.broadcasted_iota(jnp.int32, (embed, cw), 0)
        want = lax.broadcasted_iota(jnp.int32, (embed, cw), 1) + dp * cw
        pick = jnp.where(spot == want, 1.0, 0.0).astype(BF16)
        mine = jnp.dot(fresh_low, pick, preferred_element_type=F32).astype(BF16)
    spread = lax.dot_general(mine, w_ref[...], (((1,), (1,)), ((), ())), preferred_element_type=F32)
    for b in range(n_dp):
        sent[b] = spread[b:b + 1, :]
    back[dp] = sent[dp]

    def e4(k, src, dst):
        return remote(sent.at[src], back.at[dst], e4_s.at[k], e4_r.at[k], {"dp": dp_at(k)})

    each_peer(n_dp, lambda k: e4(k, dp_at(k), dp).start())

    coeffs, unused = pair_terms(
        nt_dot(low[rows:], low_fresh), back_same, None, temper, offset)
    added = jnp.dot(coeffs, low_fresh, preferred_element_type=F32)
    text_dir = direction[rows:] + added
    unit_text = unit[rows:]
    tgrad_out[...] = (
        text_dir - unit_text * jnp.sum(unit_text * text_dir, axis=1, keepdims=True)
    ) * norm[rows:]
    unit_image, image_dir = unit[:rows], direction[:rows]
    image_grad = (
        image_dir - unit_image * jnp.sum(unit_image * image_dir, axis=1, keepdims=True)
    ) * norm[:rows]
    is_fresh = (lax.broadcasted_iota(jnp.int32, (rows, 1), 0) == 0) & (mp == 0)
    fresh[...] = fresh_grad
    igrad_out[...] = jnp.where(is_fresh, fresh[pl.ds(dp, 1), :], image_grad)
    is_mine = lax.broadcasted_iota(jnp.int32, (n_dp, 1), 0) == dp
    my_loss = jnp.sum(jnp.where(is_mine, fresh_loss, 0.0), axis=0, keepdims=True)
    row_loss = jnp.where(is_fresh, my_loss, losses[:rows])
    loss_out[...] = jnp.broadcast_to(row_loss, (rows, 128)).T[0:1, :]

    for h in range(heads):
        keep(h).wait()
    each_peer(n_mp, lambda k: za(k, mp).wait_send())
    each_peer(n_q, lambda k: xb(k, dp).wait_send())
    cc(0, dp).wait_send()
    each_peer(n_q, lambda k: cc(k, chip_from(k)).wait_send())
    each_peer(n_dp, lambda k: e2(k, dp).wait_send())
    each_peer(n_mp, lambda k: e3(k, mp).wait_send())
    each_peer(n_dp, lambda k: e5(k, dp).wait_send())
    each_peer(n_dp, lambda k: e4(k, dp_at(k), dp_from(k)).wait_recv())
    total = jnp.sum(back[...], axis=0)
    cot_out[...] = (total * (LOSS_SCALE / seq)).astype(BF16).astype(F32)
    each_peer(n_dp, lambda k: e4(k, dp_at(k), dp).wait_send())


def backward_kernel(
    group,
    q_ref, k_ref, v_ref, p_ref, last_ref, cot_ref, igrad_ref, tgrad_ref, loss_ref,
    qg_ref, kg_ref, vg_ref, igrad_out, tgrad_out, loss_out,
):
    main = q_ref.shape[1] - 1
    start = pl.program_id(0) * group

    @pl.when(pl.program_id(0) == 0)
    def _():
        igrad_out[...] = igrad_ref[...]
        tgrad_out[...] = tgrad_ref[...]
        loss_out[...] = loss_ref[...]

    last_p = last_ref[...]
    last_low = last_p.astype(BF16)
    last_grad = nt_dot(v_ref[0], spread_heads(cot_ref[...], start))
    centre = jnp.sum(last_p * last_grad, axis=0, keepdims=True)
    last_score = (last_p * (last_grad - centre)).astype(BF16)
    last_query = spread_heads(q_ref[0, main:, :], start)
    qg_ref[0, main:, :] = (sum_heads(last_score, k_ref[0], start) * INV_ROOT).astype(BF16)
    head_row = lax.broadcasted_iota(jnp.int32, (HEAD_ROWS, HEAD_DIM), 0)

    for h in range(group):
        at = slice(h * HEAD_DIM, (h + 1) * HEAD_DIM)
        p = p_ref[h]
        cot = cot_ref[:, at]
        repeated = jnp.broadcast_to(cot, (HEAD_DIM, HEAD_DIM)).astype(BF16)
        prob_grad = nt_dot(v_ref[0, :, at], repeated)
        prob_grad = jnp.concatenate([prob_grad] * (main // HEAD_DIM), axis=1)
        centre = jnp.sum(p * prob_grad, axis=0, keepdims=True)
        score_grad = (p * (prob_grad - centre)).astype(BF16)
        qg_ref[0, :main, at] = (lax.dot_general(
            score_grad, k_ref[0, :, at], (((0,), (0,)), ((), ())), preferred_element_type=F32
        ) * INV_ROOT).astype(BF16)
        kg_ref[0, :, at] = ((
            jnp.dot(score_grad, q_ref[0, :main, at], preferred_element_type=F32)
            + jnp.dot(last_score, last_query[:, at], preferred_element_type=F32)
        ) * INV_ROOT).astype(BF16)
        pick = jnp.where(head_row == start + h, 1.0, 0.0).astype(BF16)
        mass = column_mass(p.astype(BF16)) + jnp.dot(
            last_low, pick, preferred_element_type=F32)
        vg_ref[0, :, at] = (mass * cot).astype(BF16)


def on_device(
    n_dp, n_mp,
    query_tokens, key_tokens, value_tokens, head_weight, image_cache, text_embed,
    text_pair, image_group, text_group, logit_scale, logit_bias,
):
    _, seq, width = query_tokens.shape
    heads = width // HEAD_DIM
    rows, embed = image_cache.shape
    cw = head_weight.shape[1]
    vmem = pl.BlockSpec(memory_space=pltpu.VMEM)
    any_space = pl.BlockSpec(memory_space=pl.ANY)
    smem = pl.BlockSpec(memory_space=pltpu.SMEM)
    n_q = n_dp // 2
    dma = pltpu.SemaphoreType.DMA
    probs, last_probs, cot, image_grad, text_grad, loss = pl.pallas_call(
        functools.partial(forward_kernel, n_dp, n_mp, heads, embed),
        out_shape=(
            jax.ShapeDtypeStruct((heads, seq, seq - 1), F32),
            jax.ShapeDtypeStruct((seq, HEAD_ROWS), F32),
            jax.ShapeDtypeStruct((1, width), F32),
            jax.ShapeDtypeStruct((rows, embed), F32),
            jax.ShapeDtypeStruct((rows, embed), F32),
            jax.ShapeDtypeStruct((1, rows), F32),
        ),
        in_specs=[any_space] * 4 + [vmem] * 2 + [smem] * 5,
        out_specs=(any_space, vmem, vmem, vmem, vmem, vmem),
        scratch_shapes=[
            pltpu.VMEM(query_tokens.shape, BF16),
            pltpu.VMEM(query_tokens.shape, BF16),
            pltpu.VMEM(query_tokens.shape, BF16),
            pltpu.VMEM(head_weight.shape, BF16),
            pltpu.VMEM((n_dp, n_mp, 2 * rows, embed + 128), BF16),
            pltpu.VMEM((n_dp, n_mp * rows, embed), BF16),
            pltpu.VMEM((heads, seq, seq - 1), F32),
            pltpu.VMEM((n_dp, 1, width), F32),
            pltpu.VMEM((n_mp, n_dp, cw), F32),
            pltpu.VMEM((n_dp, n_dp, cw), F32),
            pltpu.VMEM((n_dp, embed), F32),
            pltpu.VMEM((n_dp, 1, width), F32),
            pltpu.VMEM((n_dp, 1, width), F32),
            dma((4,)),
            dma((heads,)),
            dma((n_mp,)), dma((n_mp,)),
            dma((n_q,)), dma((n_q,)),
            dma((n_q,)), dma((n_q,)),
            dma((n_dp,)), dma((n_dp,)),
            dma((n_mp,)), dma((n_mp,)),
            dma((n_dp,)), dma((n_dp,)),
            dma((n_dp,)), dma((n_dp,)),
        ],
        compiler_params=pltpu.CompilerParams(
            collective_id=0, has_side_effects=True, vmem_limit_bytes=56 * 2**20),
        name="forward_pairs",
    )(
        query_tokens, key_tokens, value_tokens, head_weight, image_cache, text_embed,
        text_pair, image_group, text_group, logit_scale.reshape(1), logit_bias.reshape(1),
    )

    group = 2 if heads % 2 == 0 else 1
    token = pl.BlockSpec((1, seq, group * HEAD_DIM), lambda h: (0, 0, h))
    whole_rows = pl.BlockSpec((rows, embed), lambda h: (0, 0))
    whole_loss = pl.BlockSpec((1, rows), lambda h: (0, 0))
    query_grad, key_grad, value_grad, image_grad, text_grad, loss = pl.pallas_call(
        functools.partial(backward_kernel, group),
        grid=(heads // group,),
        out_shape=(
            jax.ShapeDtypeStruct(query_tokens.shape, BF16),
            jax.ShapeDtypeStruct(query_tokens.shape, BF16),
            jax.ShapeDtypeStruct(query_tokens.shape, BF16),
            jax.ShapeDtypeStruct((rows, embed), F32),
            jax.ShapeDtypeStruct((rows, embed), F32),
            jax.ShapeDtypeStruct((1, rows), F32),
        ),
        in_specs=[
            token, token, token,
            pl.BlockSpec((group, seq, seq - 1), lambda h: (h, 0, 0)),
            pl.BlockSpec((seq, HEAD_ROWS), lambda h: (0, 0)),
            pl.BlockSpec((1, group * HEAD_DIM), lambda h: (0, h)),
            whole_rows, whole_rows, whole_loss,
        ],
        out_specs=(token, token, token, whole_rows, whole_rows, whole_loss),
        compiler_params=pltpu.CompilerParams(vmem_limit_bytes=56 * 2**20),
        name="attention_back",
    )(query_tokens, key_tokens, value_tokens, probs, last_probs, cot, image_grad, text_grad, loss)
    return query_grad, key_grad, value_grad, image_grad, text_grad, loss.reshape(rows)


def solution(mesh):
    pair_rows = P(("dp", "mp"), None)
    pair = P(("dp", "mp"))
    tokens = P("dp", None, "mp")
    return jax.shard_map(
        functools.partial(on_device, mesh.shape["dp"], mesh.shape["mp"]),
        mesh=mesh,
        in_specs=(
            tokens, tokens, tokens, P("mp", "dp"), pair_rows, pair_rows, pair, pair, pair, P(), P(),
        ),
        out_specs=(tokens, tokens, tokens, pair_rows, pair_rows, pair),
        check_vma=False,
    )
```

```python
import functools
import math

import jax
import jax.numpy as jnp
from jax import lax
from jax.experimental import pallas as pl
from jax.experimental.pallas import tpu as pltpu
from jax.sharding import PartitionSpec as P

HEAD_DIM = 128
LOSS_SCALE = 8192.0
INV_ROOT = 1.0 / math.sqrt(HEAD_DIM)
F32 = jnp.float32
BF16 = jnp.bfloat16
LABEL_BASE = 64
HEAD_ROWS = 16
LOG2_E = 1.0 / math.log(2.0)


def each_peer(count, body):
    if count <= 8:
        for k in range(1, count):
            body(k)
    else:
        lax.fori_loop(1, count, lambda k, c: (body(k), c)[1], 0)


def softmax_t(scores):
    top = jnp.max(scores, axis=0, keepdims=True)
    grown = jnp.exp2((scores - top) * (INV_ROOT * LOG2_E))
    return grown * (1.0 / jnp.sum(grown, axis=0, keepdims=True))


def column_mass(probs_low):
    ones = jnp.ones((probs_low.shape[1], HEAD_DIM), BF16)
    return jnp.dot(probs_low, ones, preferred_element_type=F32)


def own_lanes(width, start=0):
    shape = (HEAD_ROWS, width)
    head = lax.broadcasted_iota(jnp.int32, shape, 0)
    return lax.broadcasted_iota(jnp.int32, shape, 1) // HEAD_DIM + start == head


def spread_heads(row, start=0):
    wide = jnp.broadcast_to(row.astype(F32), (HEAD_ROWS, row.shape[1]))
    return jnp.where(own_lanes(row.shape[1], start), wide, 0.0).astype(BF16)


def sum_heads(left, right, start=0):
    full = lax.dot_general(left, right, (((0,), (0,)), ((), ())), preferred_element_type=F32)
    own = own_lanes(right.shape[1], start)
    return jnp.sum(jnp.where(own, full, 0.0), axis=0, keepdims=True)


def pair_terms(scores, same, valid, temper, offset):
    logits = temper * scores + offset
    signed = jnp.where(same, 1.0, -1.0)
    margin = signed * logits
    tail = jnp.exp(-jnp.abs(margin))
    log_sig = jnp.minimum(margin, 0.0) - jnp.log1p(tail)
    against = jnp.where(margin >= 0, tail, 1.0) / (1.0 + tail)
    coeffs = temper * (-signed * against)
    if valid is not None:
        log_sig = jnp.where(valid, log_sig, 0.0)
        coeffs = jnp.where(valid, coeffs, 0.0)
    return coeffs.astype(BF16), -jnp.sum(log_sig, axis=1, keepdims=True)


def row_labels(tags):
    return tags[:, 0:1] * LABEL_BASE + tags[:, 1:2], tags[:, 2:3] * LABEL_BASE + tags[:, 3:4]


def lane_labels(tags):
    turned = tags.T
    return (turned[0:1, :] * LABEL_BASE + turned[1:2, :],
            turned[2:3, :] * LABEL_BASE + turned[3:4, :])


def nt_dot(left, right):
    return lax.dot_general(left, right, (((1,), (1,)), ((), ())), preferred_element_type=F32)


def forward_kernel(
    n_dp, n_mp, heads, embed,
    q_in, k_in, v_in, w_in, img_ref, txt_ref, tpair_ref, igroup_ref, tgroup_ref, scale_ref, bias_ref,
    p_out, last_out, cot_out, igrad_out, tgrad_out, loss_out,
    q_ref, k_ref, v_ref, w_ref, tslots, islots, table, probs, pooled, part, cols, fresh, sent, back,
    in_sem, p_sem, za_s, za_r, xb_s, xb_r, cc_s, cc_r, iza_s, iza_r, ixb_s, ixb_r, icc_s, icc_r, e2_s, e2_r, e3_s, e3_r, e5_s, e5_r, e4_s, e4_r,
):
    dp = lax.axis_index("dp")
    mp = lax.axis_index("mp")
    n_q = n_dp // 2
    core = lax.rem(dp, 2)
    q_me = dp // 2
    sibling = dp + 1 - 2 * core
    rows = img_ref.shape[0]
    seq = q_ref.shape[1]
    main = seq - 1
    cw = w_ref.shape[1]

    def dp_at(k):
        return lax.rem(dp + k, n_dp)

    def dp_from(k):
        return lax.rem(dp + n_dp - k, n_dp)

    def mp_at(k):
        return lax.rem(mp + k, n_mp)

    def mp_from(k):
        return lax.rem(mp + n_mp - k, n_mp)

    def chip_at(k):
        return 2 * lax.rem(q_me + k, n_q) + core

    def chip_from(k):
        return 2 * lax.rem(q_me + n_q - k, n_q) + core

    loads = [
        pltpu.make_async_copy(src, dst, in_sem.at[i])
        for i, (src, dst) in enumerate(
            ((q_in, q_ref), (k_in, k_ref), (v_in, v_ref), (w_in, w_ref)))
    ]
    for load in loads:
        load.start()
    barrier = pltpu.get_barrier_semaphore()
    each_peer(n_mp, lambda k: pl.semaphore_signal(
        barrier, inc=1, device_id={"mp": mp_at(k)}, device_id_type=pl.DeviceIdType.MESH))
    each_peer(n_dp, lambda k: pl.semaphore_signal(
        barrier, inc=1, device_id={"dp": dp_at(k)}, device_id_type=pl.DeviceIdType.MESH))

    raw = jnp.concatenate([img_ref[...].astype(F32), txt_ref[...].astype(F32)], axis=0)
    norm = lax.rsqrt(jnp.sum(raw * raw, axis=1, keepdims=True) + 1e-06)
    unit = raw * norm
    half = embed // 2
    spot = lax.broadcasted_iota(jnp.int32, (2 * rows, 128), 0)
    lane = lax.broadcasted_iota(jnp.int32, (2 * rows, 128), 1)
    first = (dp * n_mp + mp) * rows + spot
    second = jnp.zeros_like(spot)
    third = jnp.zeros_like(spot)
    for r in range(rows):
        first = jnp.where(spot == rows + r, tpair_ref[r], first)
        second = jnp.where(spot == r, igroup_ref[r], second)
        second = jnp.where(spot == rows + r, tgroup_ref[r], second)
        third = jnp.where(spot == rows + r, igroup_ref[r], third)
    label = jnp.where(lane < 2, first, jnp.where(lane < 4, second, third))
    own_tags = jnp.where(lax.rem(lane, 2) == 0, label // LABEL_BASE, lax.rem(label, LABEL_BASE))
    own_tags = own_tags.astype(F32)

    for slots, lo in ((islots, 0), (tslots, rows)):
        mine = unit[lo:lo + rows]
        slots[dp, mp, :, :half] = jnp.concatenate(
            [mine[:, :half], mine[:, half:]], axis=0).astype(BF16)
        tags = own_tags[lo:lo + rows]
        slots[dp, mp, :, half:] = jnp.concatenate([tags, tags], axis=0).astype(BF16)
    pl.semaphore_wait(barrier, n_mp - 1 + n_dp - 1)

    def remote(src, dst, s_sem, r_sem, target):
        return pltpu.make_async_remote_copy(
            src_ref=src, dst_ref=dst, send_sem=s_sem, recv_sem=r_sem,
            device_id=target, device_id_type=pl.DeviceIdType.MESH)

    def spread(slots, za_s, za_r, xb_s, xb_r, cc_s, cc_r):
        def za(k, slot):
            at = slots.at[dp, slot]
            return remote(at, at, za_s.at[k], za_r.at[k], {"mp": mp_at(k)})

        def xb(k, block):
            return remote(slots.at[block], slots.at[block], xb_s.at[k], xb_r.at[k], {"dp": chip_at(k)})

        def cc(k, block):
            return remote(slots.at[block], slots.at[block], cc_s.at[k], cc_r.at[k], {"dp": sibling})

        def along():
            each_peer(n_mp, lambda k: za(k, mp_from(k)).wait_recv())
            each_peer(n_q, lambda k: xb(k, dp).start())
            cc(0, dp).start()

        def relay(k):
            xb(k, chip_from(k)).wait_recv()
            cc(k, chip_from(k)).start()

        def settle(k):
            block = 2 * lax.rem(q_me + n_q - k, n_q) + 1 - core
            cc(k, block).wait_recv()

        def settle_all():
            settle(0)
            each_peer(n_q, settle)

        def drain():
            each_peer(n_mp, lambda k: za(k, mp).wait_send())
            each_peer(n_q, lambda k: xb(k, dp).wait_send())
            cc(0, dp).wait_send()
            each_peer(n_q, lambda k: cc(k, chip_from(k)).wait_send())

        begin = lambda: each_peer(n_mp, lambda k: za(k, mp).start())
        return begin, along, lambda: each_peer(n_q, relay), settle_all, drain

    t_begin, t_along, t_relay, t_settle, t_drain = spread(
        tslots, za_s, za_r, xb_s, xb_r, cc_s, cc_r)
    i_begin, i_along, i_relay, i_settle, i_drain = spread(
        islots, iza_s, iza_r, ixb_s, ixb_r, icc_s, icc_r)

    t_begin()
    i_begin()

    for load in loads[:3]:
        load.wait()

    last_p = softmax_t(nt_dot(k_ref[0], spread_heads(q_ref[0, main:, :])))
    last_out[...] = last_p
    last_mean = sum_heads(last_p.astype(BF16), v_ref[0])

    def head(h):
        at = pl.ds(pl.multiple_of(h * HEAD_DIM, HEAD_DIM), HEAD_DIM)
        p = softmax_t(nt_dot(k_ref[0, :, at], q_ref[0, :main, at]))
        probs[h] = p
        mass = column_mass(p.astype(BF16))
        pooled[dp, :, at] = jnp.sum(mass * v_ref[0, :, at].astype(F32), axis=0, keepdims=True)

    def keep(h):
        return pltpu.make_async_copy(probs.at[h], p_out.at[h], p_sem.at[h])

    group = 2 if heads % 2 == 0 else 1

    def some_heads(i, carry):
        for u in range(group):
            head(i * group + u)

        @pl.when(i == 1)
        def _():
            t_along()

        return carry

    lax.fori_loop(0, heads // group, some_heads, 0)
    mean = (pooled[dp] + last_mean) * (1.0 / seq)
    pooled[dp] = mean.astype(BF16).astype(F32)

    def e2(k, slot):
        return remote(pooled.at[slot], pooled.at[slot], e2_s.at[k], e2_r.at[k], {"dp": dp_at(k)})

    each_peer(n_dp, lambda k: e2(k, dp).start())
    i_along()
    for h in range(heads):
        keep(h).start()
    t_relay()
    loads[3].wait()
    each_peer(n_dp, lambda k: e2(k, dp_from(k)).wait_recv())
    every = pooled[...].reshape(n_dp, heads * HEAD_DIM).astype(BF16)
    part[mp] = jnp.dot(every, w_ref[...], preferred_element_type=F32)

    def e3(k, slot):
        return remote(part.at[slot], part.at[slot], e3_s.at[k], e3_r.at[k], {"mp": mp_at(k)})

    each_peer(n_mp, lambda k: e3(k, mp).start())

    each_peer(n_mp, lambda k: e3(k, mp_from(k)).wait_recv())
    cols[dp] = jnp.sum(part[...], axis=0)

    def e5(k, slot):
        return remote(cols.at[slot], cols.at[slot], e5_s.at[k], e5_r.at[k], {"dp": dp_at(k)})

    each_peer(n_dp, lambda k: e5(k, dp).start())

    t_settle()

    def gather(slots, whole, b):
        wide = slots[b].astype(F32)
        left = wide[:, :rows, :half].reshape(n_mp * rows, half)
        right = wide[:, rows:, :half].reshape(n_mp * rows, half)
        whole[b] = jnp.concatenate([left, right], axis=1).astype(BF16)

    def gather_all(slots, whole):
        gather(slots, whole, 0)
        each_peer(n_dp, lambda b: gather(slots, whole, b))

    def tags_of(slots):
        return slots[:, :, :, half:].astype(F32)[:, :, :rows].reshape(n_dp * n_mp * rows, 128)

    def all_rows():
        return table[...].reshape(n_dp * n_mp * rows, embed)

    gather_all(tslots, table)
    low = unit.astype(BF16)
    unit_image, unit_text = unit[:rows], unit[rows:]
    temper = jnp.exp(jnp.full((1, 1), scale_ref[0], F32))
    offset = bias_ref[0]
    own_a, own_b = row_labels(own_tags)
    text_a, text_b = lane_labels(tags_of(tslots))
    coeffs, losses = pair_terms(
        nt_dot(low[:rows], all_rows()),
        (own_a[:rows] == text_a) | (own_b[:rows] == text_b), None, temper, offset)
    image_dir = jnp.dot(coeffs, all_rows(), preferred_element_type=F32)
    image_grad = (
        image_dir - unit_image * jnp.sum(unit_image * image_dir, axis=1, keepdims=True)
    ) * norm[:rows]
    i_relay()

    tags = tslots[:, 0, :, half:].astype(F32)
    lead = lax.broadcasted_iota(jnp.int32, tags.shape, 1) == 0
    fresh_tags = jnp.sum(jnp.where(lead, tags, 0.0), axis=1)
    fresh_a = (lax.broadcasted_iota(jnp.int32, (n_dp, 1), 0) * (n_mp * rows)).astype(F32)
    fresh_b = fresh_tags[:, 4:5] * LABEL_BASE + fresh_tags[:, 5:6]
    fresh_same = (fresh_a == text_a) | (fresh_b == text_b)
    each_peer(n_dp, lambda k: e5(k, dp_from(k)).wait_recv())
    for c in range(n_dp):
        fresh[:, c * cw:(c + 1) * cw] = cols[c]
    raw_fresh = fresh[...]
    fresh_norm = lax.rsqrt(jnp.sum(raw_fresh * raw_fresh, axis=1, keepdims=True) + 1e-06)
    unit_fresh = raw_fresh * fresh_norm
    low_fresh = unit_fresh.astype(BF16)
    coeffs, fresh_loss = pair_terms(
        nt_dot(low_fresh, all_rows()), fresh_same, None, temper, offset)
    fresh_dir = jnp.dot(coeffs, all_rows(), preferred_element_type=F32)
    fresh_grad = (
        fresh_dir - unit_fresh * jnp.sum(unit_fresh * fresh_dir, axis=1, keepdims=True)
    ) * fresh_norm
    fresh_low = fresh_grad.astype(BF16)

    if cw % 128 == 0:
        fresh[...] = fresh_low.astype(F32)
        mine = fresh[:, pl.ds(pl.multiple_of(dp * cw, 128), cw)].astype(BF16)
    else:
        spot = lax.broadcasted_iota(jnp.int32, (embed, cw), 0)
        want = lax.broadcasted_iota(jnp.int32, (embed, cw), 1) + dp * cw
        pick = jnp.where(spot == want, 1.0, 0.0).astype(BF16)
        mine = jnp.dot(fresh_low, pick, preferred_element_type=F32).astype(BF16)
    spread = lax.dot_general(mine, w_ref[...], (((1,), (1,)), ((), ())), preferred_element_type=F32)
    for b in range(n_dp):
        sent[b] = spread[b:b + 1, :]
    back[dp] = sent[dp]

    def e4(k, src, dst):
        return remote(sent.at[src], back.at[dst], e4_s.at[k], e4_r.at[k], {"dp": dp_at(k)})

    each_peer(n_dp, lambda k: e4(k, dp_at(k), dp).start())

    i_settle()
    gather_all(islots, table)
    image_a, image_b = lane_labels(tags_of(islots))
    fresh_lane_a = (lax.broadcasted_iota(jnp.int32, (1, n_dp), 1) * (n_mp * rows)).astype(F32)
    fresh_turned = fresh_tags.T
    fresh_lane_b = fresh_turned[4:5] * LABEL_BASE + fresh_turned[5:6]
    stale = lax.rem(
        lax.broadcasted_iota(jnp.int32, (1, n_dp * n_mp * rows), 1), n_mp * rows) == 0
    coeffs, unused = pair_terms(
        nt_dot(low[rows:], all_rows()),
        (own_a[rows:] == image_a) | (own_b[rows:] == image_b),
        jnp.logical_not(stale), temper, offset)
    text_dir = jnp.dot(coeffs, all_rows(), preferred_element_type=F32)
    coeffs, unused = pair_terms(
        nt_dot(low[rows:], low_fresh),
        (own_a[rows:] == fresh_lane_a) | (own_b[rows:] == fresh_lane_b), None, temper, offset)
    text_dir = text_dir + jnp.dot(coeffs, low_fresh, preferred_element_type=F32)
    tgrad_out[...] = (
        text_dir - unit_text * jnp.sum(unit_text * text_dir, axis=1, keepdims=True)
    ) * norm[rows:]
    is_fresh = (lax.broadcasted_iota(jnp.int32, (rows, 1), 0) == 0) & (mp == 0)
    fresh[...] = fresh_grad
    igrad_out[...] = jnp.where(is_fresh, fresh[pl.ds(dp, 1), :], image_grad)
    is_mine = lax.broadcasted_iota(jnp.int32, (n_dp, 1), 0) == dp
    my_loss = jnp.sum(jnp.where(is_mine, fresh_loss, 0.0), axis=0, keepdims=True)
    row_loss = jnp.where(is_fresh, my_loss, losses[:rows])
    loss_out[...] = jnp.broadcast_to(row_loss, (rows, 128)).T[0:1, :]

    for h in range(heads):
        keep(h).wait()
    t_drain()
    i_drain()
    each_peer(n_dp, lambda k: e2(k, dp).wait_send())
    each_peer(n_mp, lambda k: e3(k, mp).wait_send())
    each_peer(n_dp, lambda k: e5(k, dp).wait_send())
    each_peer(n_dp, lambda k: e4(k, dp_at(k), dp_from(k)).wait_recv())
    total = jnp.sum(back[...], axis=0)
    cot_out[...] = (total * (LOSS_SCALE / seq)).astype(BF16).astype(F32)
    each_peer(n_dp, lambda k: e4(k, dp_at(k), dp).wait_send())


def backward_kernel(
    group,
    q_ref, k_ref, v_ref, p_ref, last_ref, cot_ref, igrad_ref, tgrad_ref, loss_ref,
    qg_ref, kg_ref, vg_ref, igrad_out, tgrad_out, loss_out,
):
    main = q_ref.shape[1] - 1
    start = pl.program_id(0) * group

    @pl.when(pl.program_id(0) == 0)
    def _():
        igrad_out[...] = igrad_ref[...]
        tgrad_out[...] = tgrad_ref[...]
        loss_out[...] = loss_ref[...]

    last_p = last_ref[...]
    last_low = last_p.astype(BF16)
    last_grad = nt_dot(v_ref[0], spread_heads(cot_ref[...], start))
    centre = jnp.sum(last_p * last_grad, axis=0, keepdims=True)
    last_score = (last_p * (last_grad - centre)).astype(BF16)
    last_query = spread_heads(q_ref[0, main:, :], start)
    qg_ref[0, main:, :] = (sum_heads(last_score, k_ref[0], start) * INV_ROOT).astype(BF16)
    head_row = lax.broadcasted_iota(jnp.int32, (HEAD_ROWS, HEAD_DIM), 0)

    for h in range(group):
        at = slice(h * HEAD_DIM, (h + 1) * HEAD_DIM)
        p = p_ref[h]
        cot = cot_ref[:, at]
        repeated = jnp.broadcast_to(cot, (HEAD_DIM, HEAD_DIM)).astype(BF16)
        prob_grad = nt_dot(v_ref[0, :, at], repeated)
        prob_grad = jnp.concatenate([prob_grad] * (main // HEAD_DIM), axis=1)
        centre = jnp.sum(p * prob_grad, axis=0, keepdims=True)
        score_grad = (p * (prob_grad - centre)).astype(BF16)
        qg_ref[0, :main, at] = (lax.dot_general(
            score_grad, k_ref[0, :, at], (((0,), (0,)), ((), ())), preferred_element_type=F32
        ) * INV_ROOT).astype(BF16)
        kg_ref[0, :, at] = ((
            jnp.dot(score_grad, q_ref[0, :main, at], preferred_element_type=F32)
            + jnp.dot(last_score, last_query[:, at], preferred_element_type=F32)
        ) * INV_ROOT).astype(BF16)
        pick = jnp.where(head_row == start + h, 1.0, 0.0).astype(BF16)
        mass = column_mass(p.astype(BF16)) + jnp.dot(
            last_low, pick, preferred_element_type=F32)
        vg_ref[0, :, at] = (mass * cot).astype(BF16)


def on_device(
    n_dp, n_mp,
    query_tokens, key_tokens, value_tokens, head_weight, image_cache, text_embed,
    text_pair, image_group, text_group, logit_scale, logit_bias,
):
    _, seq, width = query_tokens.shape
    heads = width // HEAD_DIM
    rows, embed = image_cache.shape
    cw = head_weight.shape[1]
    vmem = pl.BlockSpec(memory_space=pltpu.VMEM)
    any_space = pl.BlockSpec(memory_space=pl.ANY)
    smem = pl.BlockSpec(memory_space=pltpu.SMEM)
    n_q = n_dp // 2
    dma = pltpu.SemaphoreType.DMA
    probs, last_probs, cot, image_grad, text_grad, loss = pl.pallas_call(
        functools.partial(forward_kernel, n_dp, n_mp, heads, embed),
        out_shape=(
            jax.ShapeDtypeStruct((heads, seq, seq - 1), F32),
            jax.ShapeDtypeStruct((seq, HEAD_ROWS), F32),
            jax.ShapeDtypeStruct((1, width), F32),
            jax.ShapeDtypeStruct((rows, embed), F32),
            jax.ShapeDtypeStruct((rows, embed), F32),
            jax.ShapeDtypeStruct((1, rows), F32),
        ),
        in_specs=[any_space] * 4 + [vmem] * 2 + [smem] * 5,
        out_specs=(any_space, vmem, vmem, vmem, vmem, vmem),
        scratch_shapes=[
            pltpu.VMEM(query_tokens.shape, BF16),
            pltpu.VMEM(query_tokens.shape, BF16),
            pltpu.VMEM(query_tokens.shape, BF16),
            pltpu.VMEM(head_weight.shape, BF16),
            pltpu.VMEM((n_dp, n_mp, 2 * rows, embed // 2 + 128), BF16),
            pltpu.VMEM((n_dp, n_mp, 2 * rows, embed // 2 + 128), BF16),
            pltpu.VMEM((n_dp, n_mp * rows, embed), BF16),
            pltpu.VMEM((heads, seq, seq - 1), F32),
            pltpu.VMEM((n_dp, 1, width), F32),
            pltpu.VMEM((n_mp, n_dp, cw), F32),
            pltpu.VMEM((n_dp, n_dp, cw), F32),
            pltpu.VMEM((n_dp, embed), F32),
            pltpu.VMEM((n_dp, 1, width), F32),
            pltpu.VMEM((n_dp, 1, width), F32),
            dma((4,)),
            dma((heads,)),
            dma((n_mp,)), dma((n_mp,)),
            dma((n_q,)), dma((n_q,)),
            dma((n_q,)), dma((n_q,)),
            dma((n_mp,)), dma((n_mp,)),
            dma((n_q,)), dma((n_q,)),
            dma((n_q,)), dma((n_q,)),
            dma((n_dp,)), dma((n_dp,)),
            dma((n_mp,)), dma((n_mp,)),
            dma((n_dp,)), dma((n_dp,)),
            dma((n_dp,)), dma((n_dp,)),
        ],
        compiler_params=pltpu.CompilerParams(
            collective_id=0, has_side_effects=True, vmem_limit_bytes=56 * 2**20),
        name="forward_pairs",
    )(
        query_tokens, key_tokens, value_tokens, head_weight, image_cache, text_embed,
        text_pair, image_group, text_group, logit_scale.reshape(1), logit_bias.reshape(1),
    )

    group = 2 if heads % 2 == 0 else 1
    token = pl.BlockSpec((1, seq, group * HEAD_DIM), lambda h: (0, 0, h))
    whole_rows = pl.BlockSpec((rows, embed), lambda h: (0, 0))
    whole_loss = pl.BlockSpec((1, rows), lambda h: (0, 0))
    query_grad, key_grad, value_grad, image_grad, text_grad, loss = pl.pallas_call(
        functools.partial(backward_kernel, group),
        grid=(heads // group,),
        out_shape=(
            jax.ShapeDtypeStruct(query_tokens.shape, BF16),
            jax.ShapeDtypeStruct(query_tokens.shape, BF16),
            jax.ShapeDtypeStruct(query_tokens.shape, BF16),
            jax.ShapeDtypeStruct((rows, embed), F32),
            jax.ShapeDtypeStruct((rows, embed), F32),
            jax.ShapeDtypeStruct((1, rows), F32),
        ),
        in_specs=[
            token, token, token,
            pl.BlockSpec((group, seq, seq - 1), lambda h: (h, 0, 0)),
            pl.BlockSpec((seq, HEAD_ROWS), lambda h: (0, 0)),
            pl.BlockSpec((1, group * HEAD_DIM), lambda h: (0, h)),
            whole_rows, whole_rows, whole_loss,
        ],
        out_specs=(token, token, token, whole_rows, whole_rows, whole_loss),
        compiler_params=pltpu.CompilerParams(vmem_limit_bytes=56 * 2**20),
        name="attention_back",
    )(query_tokens, key_tokens, value_tokens, probs, last_probs, cot, image_grad, text_grad, loss)
    return query_grad, key_grad, value_grad, image_grad, text_grad, loss.reshape(rows)


def solution(mesh):
    pair_rows = P(("dp", "mp"), None)
    pair = P(("dp", "mp"))
    tokens = P("dp", None, "mp")
    return jax.shard_map(
        functools.partial(on_device, mesh.shape["dp"], mesh.shape["mp"]),
        mesh=mesh,
        in_specs=(
            tokens, tokens, tokens, P("mp", "dp"), pair_rows, pair_rows, pair, pair, pair, P(), P(),
        ),
        out_specs=(tokens, tokens, tokens, pair_rows, pair_rows, pair),
        check_vma=False,
    )
```

```python
import functools
import math

import jax
import jax.numpy as jnp
from jax import lax
from jax.experimental import pallas as pl
from jax.experimental.pallas import tpu as pltpu
from jax.sharding import PartitionSpec as P

HEAD_DIM = 128
LOSS_SCALE = 8192.0
INV_ROOT = 1.0 / math.sqrt(HEAD_DIM)
F32 = jnp.float32
BF16 = jnp.bfloat16
LABEL_BASE = 64
HEAD_ROWS = 16
LOG2_E = 1.0 / math.log(2.0)


def each_peer(count, body):
    if count <= 8:
        for k in range(1, count):
            body(k)
    else:
        lax.fori_loop(1, count, lambda k, c: (body(k), c)[1], 0)


def softmax_t(scores):
    top = jnp.max(scores, axis=0, keepdims=True)
    grown = jnp.exp2((scores - top) * (INV_ROOT * LOG2_E))
    return grown * (1.0 / jnp.sum(grown, axis=0, keepdims=True))


def column_mass(probs_low):
    return jnp.sum(probs_low.astype(F32), axis=1, keepdims=True)


def own_lanes(width, start=0):
    shape = (HEAD_ROWS, width)
    head = lax.broadcasted_iota(jnp.int32, shape, 0)
    return lax.broadcasted_iota(jnp.int32, shape, 1) // HEAD_DIM + start == head


def spread_heads(row, start=0):
    wide = jnp.broadcast_to(row.astype(F32), (HEAD_ROWS, row.shape[1]))
    return jnp.where(own_lanes(row.shape[1], start), wide, 0.0).astype(BF16)


def sum_heads(left, right, start=0):
    full = lax.dot_general(left, right, (((0,), (0,)), ((), ())), preferred_element_type=F32)
    own = own_lanes(right.shape[1], start)
    return jnp.sum(jnp.where(own, full, 0.0), axis=0, keepdims=True)


def pair_terms(scores, same, valid, temper, offset):
    logits = temper * scores + offset
    signed = jnp.where(same, 1.0, -1.0)
    margin = signed * logits
    tail = jnp.exp(-jnp.abs(margin))
    log_sig = jnp.minimum(margin, 0.0) - jnp.log1p(tail)
    against = jnp.where(margin >= 0, tail, 1.0) / (1.0 + tail)
    coeffs = temper * (-signed * against)
    if valid is not None:
        log_sig = jnp.where(valid, log_sig, 0.0)
        coeffs = jnp.where(valid, coeffs, 0.0)
    return coeffs.astype(BF16), -jnp.sum(log_sig, axis=1, keepdims=True)


def row_labels(tags):
    return tags[:, 0:1] * LABEL_BASE + tags[:, 1:2], tags[:, 2:3] * LABEL_BASE + tags[:, 3:4]


def lane_labels(tags):
    turned = tags.T
    return (turned[0:1, :] * LABEL_BASE + turned[1:2, :],
            turned[2:3, :] * LABEL_BASE + turned[3:4, :])


def nt_dot(left, right):
    return lax.dot_general(left, right, (((1,), (1,)), ((), ())), preferred_element_type=F32)


def forward_kernel(
    n_dp, n_mp, heads, embed,
    q_in, k_in, v_in, w_in, img_ref, txt_ref, tpair_ref, igroup_ref, tgroup_ref, scale_ref, bias_ref,
    p_out, last_out, cot_out, igrad_out, tgrad_out, loss_out,
    q_ref, k_ref, v_ref, w_ref, tslots, islots, table, probs, pooled, part, cols, fresh, sent, back,
    in_sem, p_sem, za_s, za_r, xb_s, xb_r, cc_s, cc_r, iza_s, iza_r, ixb_s, ixb_r, icc_s, icc_r, e2_s, e2_r, e3_s, e3_r, e5_s, e5_r, e4_s, e4_r,
):
    dp = lax.axis_index("dp")
    mp = lax.axis_index("mp")
    n_q = n_dp // 2
    core = lax.rem(dp, 2)
    q_me = dp // 2
    sibling = dp + 1 - 2 * core
    rows = img_ref.shape[0]
    seq = q_ref.shape[1]
    main = seq - 1
    cw = w_ref.shape[1]

    def dp_at(k):
        return lax.rem(dp + k, n_dp)

    def dp_from(k):
        return lax.rem(dp + n_dp - k, n_dp)

    def mp_at(k):
        return lax.rem(mp + k, n_mp)

    def mp_from(k):
        return lax.rem(mp + n_mp - k, n_mp)

    def chip_at(k):
        return 2 * lax.rem(q_me + k, n_q) + core

    def chip_from(k):
        return 2 * lax.rem(q_me + n_q - k, n_q) + core

    loads = [
        pltpu.make_async_copy(src, dst, in_sem.at[i])
        for i, (src, dst) in enumerate(
            ((q_in, q_ref), (k_in, k_ref), (v_in, v_ref), (w_in, w_ref)))
    ]
    for load in loads:
        load.start()
    barrier = pltpu.get_barrier_semaphore()
    each_peer(n_mp, lambda k: pl.semaphore_signal(
        barrier, inc=1, device_id={"mp": mp_at(k)}, device_id_type=pl.DeviceIdType.MESH))
    each_peer(n_dp, lambda k: pl.semaphore_signal(
        barrier, inc=1, device_id={"dp": dp_at(k)}, device_id_type=pl.DeviceIdType.MESH))

    raw = jnp.concatenate([img_ref[...].astype(F32), txt_ref[...].astype(F32)], axis=0)
    norm = lax.rsqrt(jnp.sum(raw * raw, axis=1, keepdims=True) + 1e-06)
    unit = raw * norm
    half = embed // 2
    spot = lax.broadcasted_iota(jnp.int32, (2 * rows, 128), 0)
    lane = lax.broadcasted_iota(jnp.int32, (2 * rows, 128), 1)
    first = (dp * n_mp + mp) * rows + spot
    second = jnp.zeros_like(spot)
    third = jnp.zeros_like(spot)
    for r in range(rows):
        first = jnp.where(spot == rows + r, tpair_ref[r], first)
        second = jnp.where(spot == r, igroup_ref[r], second)
        second = jnp.where(spot == rows + r, tgroup_ref[r], second)
        third = jnp.where(spot == rows + r, igroup_ref[r], third)
    label = jnp.where(lane < 2, first, jnp.where(lane < 4, second, third))
    own_tags = jnp.where(lax.rem(lane, 2) == 0, label // LABEL_BASE, lax.rem(label, LABEL_BASE))
    own_tags = own_tags.astype(F32)

    for slots, lo in ((islots, 0), (tslots, rows)):
        mine = unit[lo:lo + rows]
        slots[dp, mp, :, :half] = jnp.concatenate(
            [mine[:, :half], mine[:, half:]], axis=0).astype(BF16)
        tags = own_tags[lo:lo + rows]
        slots[dp, mp, :, half:] = jnp.concatenate([tags, tags], axis=0).astype(BF16)
    pl.semaphore_wait(barrier, n_mp - 1 + n_dp - 1)

    def remote(src, dst, s_sem, r_sem, target):
        return pltpu.make_async_remote_copy(
            src_ref=src, dst_ref=dst, send_sem=s_sem, recv_sem=r_sem,
            device_id=target, device_id_type=pl.DeviceIdType.MESH)

    def spread(slots, za_s, za_r, xb_s, xb_r, cc_s, cc_r):
        def za(k, slot):
            at = slots.at[dp, slot]
            return remote(at, at, za_s.at[k], za_r.at[k], {"mp": mp_at(k)})

        def xb(k, block):
            return remote(slots.at[block], slots.at[block], xb_s.at[k], xb_r.at[k], {"dp": chip_at(k)})

        def cc(k, block):
            return remote(slots.at[block], slots.at[block], cc_s.at[k], cc_r.at[k], {"dp": sibling})

        def along():
            each_peer(n_mp, lambda k: za(k, mp_from(k)).wait_recv())
            each_peer(n_q, lambda k: xb(k, dp).start())
            cc(0, dp).start()

        def relay(k):
            xb(k, chip_from(k)).wait_recv()
            cc(k, chip_from(k)).start()

        def settle(k):
            block = 2 * lax.rem(q_me + n_q - k, n_q) + 1 - core
            cc(k, block).wait_recv()

        def settle_all():
            settle(0)
            each_peer(n_q, settle)

        def drain():
            each_peer(n_mp, lambda k: za(k, mp).wait_send())
            each_peer(n_q, lambda k: xb(k, dp).wait_send())
            cc(0, dp).wait_send()
            each_peer(n_q, lambda k: cc(k, chip_from(k)).wait_send())

        begin = lambda: each_peer(n_mp, lambda k: za(k, mp).start())
        return begin, along, lambda: each_peer(n_q, relay), settle_all, drain

    t_begin, t_along, t_relay, t_settle, t_drain = spread(
        tslots, za_s, za_r, xb_s, xb_r, cc_s, cc_r)
    i_begin, i_along, i_relay, i_settle, i_drain = spread(
        islots, iza_s, iza_r, ixb_s, ixb_r, icc_s, icc_r)

    t_begin()
    i_begin()

    for load in loads[:3]:
        load.wait()

    last_p = softmax_t(nt_dot(k_ref[0], spread_heads(q_ref[0, main:, :])))
    last_out[...] = last_p
    last_mean = sum_heads(last_p.astype(BF16), v_ref[0])

    def head(h):
        at = pl.ds(pl.multiple_of(h * HEAD_DIM, HEAD_DIM), HEAD_DIM)
        p = softmax_t(nt_dot(k_ref[0, :, at], q_ref[0, :main, at]))
        probs[h] = p
        mass = column_mass(p.astype(BF16))
        pooled[dp, :, at] = jnp.sum(mass * v_ref[0, :, at].astype(F32), axis=0, keepdims=True)

    def keep(h):
        return pltpu.make_async_copy(probs.at[h], p_out.at[h], p_sem.at[h])

    group = 2 if heads % 2 == 0 else 1

    def some_heads(i, carry):
        for u in range(group):
            head(i * group + u)

        @pl.when(i == 1)
        def _():
            t_along()

        return carry

    lax.fori_loop(0, heads // group, some_heads, 0)
    mean = (pooled[dp] + last_mean) * (1.0 / seq)
    pooled[dp] = mean.astype(BF16).astype(F32)

    def e2(k, slot):
        return remote(pooled.at[slot], pooled.at[slot], e2_s.at[k], e2_r.at[k], {"dp": dp_at(k)})

    each_peer(n_dp, lambda k: e2(k, dp).start())
    i_along()
    for h in range(heads):
        keep(h).start()
    t_relay()
    loads[3].wait()
    each_peer(n_dp, lambda k: e2(k, dp_from(k)).wait_recv())
    every = pooled[...].reshape(n_dp, heads * HEAD_DIM).astype(BF16)
    part[mp] = jnp.dot(every, w_ref[...], preferred_element_type=F32)

    def e3(k, slot):
        return remote(part.at[slot], part.at[slot], e3_s.at[k], e3_r.at[k], {"mp": mp_at(k)})

    each_peer(n_mp, lambda k: e3(k, mp).start())

    each_peer(n_mp, lambda k: e3(k, mp_from(k)).wait_recv())
    cols[dp] = jnp.sum(part[...], axis=0)

    def e5(k, slot):
        return remote(cols.at[slot], cols.at[slot], e5_s.at[k], e5_r.at[k], {"dp": dp_at(k)})

    each_peer(n_dp, lambda k: e5(k, dp).start())

    t_settle()

    def gather(slots, whole, b):
        wide = slots[b].astype(F32)
        left = wide[:, :rows, :half].reshape(n_mp * rows, half)
        right = wide[:, rows:, :half].reshape(n_mp * rows, half)
        whole[b] = jnp.concatenate([left, right], axis=1).astype(BF16)

    def gather_all(slots, whole):
        gather(slots, whole, 0)
        each_peer(n_dp, lambda b: gather(slots, whole, b))

    def tags_of(slots):
        return slots[:, :, :, half:].astype(F32)[:, :, :rows].reshape(n_dp * n_mp * rows, 128)

    def all_rows():
        return table[...].reshape(n_dp * n_mp * rows, embed)

    gather_all(tslots, table)
    low = unit.astype(BF16)
    unit_image, unit_text = unit[:rows], unit[rows:]
    temper = jnp.exp(jnp.full((1, 1), scale_ref[0], F32))
    offset = bias_ref[0]
    own_a, own_b = row_labels(own_tags)
    text_a, text_b = lane_labels(tags_of(tslots))
    coeffs, losses = pair_terms(
        nt_dot(low[:rows], all_rows()),
        (own_a[:rows] == text_a) | (own_b[:rows] == text_b), None, temper, offset)
    image_dir = jnp.dot(coeffs, all_rows(), preferred_element_type=F32)
    image_grad = (
        image_dir - unit_image * jnp.sum(unit_image * image_dir, axis=1, keepdims=True)
    ) * norm[:rows]
    i_relay()

    tags = tslots[:, 0, :, half:].astype(F32)
    lead = lax.broadcasted_iota(jnp.int32, tags.shape, 1) == 0
    fresh_tags = jnp.sum(jnp.where(lead, tags, 0.0), axis=1)
    fresh_a = (lax.broadcasted_iota(jnp.int32, (n_dp, 1), 0) * (n_mp * rows)).astype(F32)
    fresh_b = fresh_tags[:, 4:5] * LABEL_BASE + fresh_tags[:, 5:6]
    fresh_same = (fresh_a == text_a) | (fresh_b == text_b)
    each_peer(n_dp, lambda k: e5(k, dp_from(k)).wait_recv())
    for c in range(n_dp):
        fresh[:, c * cw:(c + 1) * cw] = cols[c]
    raw_fresh = fresh[...]
    fresh_norm = lax.rsqrt(jnp.sum(raw_fresh * raw_fresh, axis=1, keepdims=True) + 1e-06)
    unit_fresh = raw_fresh * fresh_norm
    low_fresh = unit_fresh.astype(BF16)
    coeffs, fresh_loss = pair_terms(
        nt_dot(low_fresh, all_rows()), fresh_same, None, temper, offset)
    fresh_dir = jnp.dot(coeffs, all_rows(), preferred_element_type=F32)
    fresh_grad = (
        fresh_dir - unit_fresh * jnp.sum(unit_fresh * fresh_dir, axis=1, keepdims=True)
    ) * fresh_norm
    fresh_low = fresh_grad.astype(BF16)

    if cw % 128 == 0:
        fresh[...] = fresh_low.astype(F32)
        mine = fresh[:, pl.ds(pl.multiple_of(dp * cw, 128), cw)].astype(BF16)
    else:
        spot = lax.broadcasted_iota(jnp.int32, (embed, cw), 0)
        want = lax.broadcasted_iota(jnp.int32, (embed, cw), 1) + dp * cw
        pick = jnp.where(spot == want, 1.0, 0.0).astype(BF16)
        mine = jnp.dot(fresh_low, pick, preferred_element_type=F32).astype(BF16)
    spread = lax.dot_general(mine, w_ref[...], (((1,), (1,)), ((), ())), preferred_element_type=F32)
    for b in range(n_dp):
        sent[b] = spread[b:b + 1, :]
    back[dp] = sent[dp]

    def e4(k, src, dst):
        return remote(sent.at[src], back.at[dst], e4_s.at[k], e4_r.at[k], {"dp": dp_at(k)})

    each_peer(n_dp, lambda k: e4(k, dp_at(k), dp).start())

    i_settle()
    gather_all(islots, table)
    image_a, image_b = lane_labels(tags_of(islots))
    fresh_lane_a = (lax.broadcasted_iota(jnp.int32, (1, n_dp), 1) * (n_mp * rows)).astype(F32)
    fresh_turned = fresh_tags.T
    fresh_lane_b = fresh_turned[4:5] * LABEL_BASE + fresh_turned[5:6]
    stale = lax.rem(
        lax.broadcasted_iota(jnp.int32, (1, n_dp * n_mp * rows), 1), n_mp * rows) == 0
    coeffs, unused = pair_terms(
        nt_dot(low[rows:], all_rows()),
        (own_a[rows:] == image_a) | (own_b[rows:] == image_b),
        jnp.logical_not(stale), temper, offset)
    text_dir = jnp.dot(coeffs, all_rows(), preferred_element_type=F32)
    coeffs, unused = pair_terms(
        nt_dot(low[rows:], low_fresh),
        (own_a[rows:] == fresh_lane_a) | (own_b[rows:] == fresh_lane_b), None, temper, offset)
    text_dir = text_dir + jnp.dot(coeffs, low_fresh, preferred_element_type=F32)
    tgrad_out[...] = (
        text_dir - unit_text * jnp.sum(unit_text * text_dir, axis=1, keepdims=True)
    ) * norm[rows:]
    is_fresh = (lax.broadcasted_iota(jnp.int32, (rows, 1), 0) == 0) & (mp == 0)
    fresh[...] = fresh_grad
    igrad_out[...] = jnp.where(is_fresh, fresh[pl.ds(dp, 1), :], image_grad)
    is_mine = lax.broadcasted_iota(jnp.int32, (n_dp, 1), 0) == dp
    my_loss = jnp.sum(jnp.where(is_mine, fresh_loss, 0.0), axis=0, keepdims=True)
    row_loss = jnp.where(is_fresh, my_loss, losses[:rows])
    loss_out[...] = jnp.broadcast_to(row_loss, (rows, 128)).T[0:1, :]

    for h in range(heads):
        keep(h).wait()
    t_drain()
    i_drain()
    each_peer(n_dp, lambda k: e2(k, dp).wait_send())
    each_peer(n_mp, lambda k: e3(k, mp).wait_send())
    each_peer(n_dp, lambda k: e5(k, dp).wait_send())
    each_peer(n_dp, lambda k: e4(k, dp_at(k), dp_from(k)).wait_recv())
    total = jnp.sum(back[...], axis=0)
    cot_out[...] = (total * (LOSS_SCALE / seq)).astype(BF16).astype(F32)
    each_peer(n_dp, lambda k: e4(k, dp_at(k), dp).wait_send())


def backward_kernel(
    group,
    q_ref, k_ref, v_ref, p_ref, last_ref, cot_ref, igrad_ref, tgrad_ref, loss_ref,
    qg_ref, kg_ref, vg_ref, igrad_out, tgrad_out, loss_out,
):
    main = q_ref.shape[1] - 1
    start = pl.program_id(0) * group

    @pl.when(pl.program_id(0) == 0)
    def _():
        igrad_out[...] = igrad_ref[...]
        tgrad_out[...] = tgrad_ref[...]
        loss_out[...] = loss_ref[...]

    last_p = last_ref[...]
    last_low = last_p.astype(BF16)
    last_grad = nt_dot(v_ref[0], spread_heads(cot_ref[...], start))
    centre = jnp.sum(last_p * last_grad, axis=0, keepdims=True)
    last_score = (last_p * (last_grad - centre)).astype(BF16)
    qg_ref[0, main:, :] = (sum_heads(last_score, k_ref[0], start) * INV_ROOT).astype(BF16)
    head_lane = lax.broadcasted_iota(jnp.int32, last_p.shape, 1)

    for h in range(group):
        at = slice(h * HEAD_DIM, (h + 1) * HEAD_DIM)
        p = p_ref[h]
        cot = cot_ref[:, at]
        mine = head_lane == start + h

        def column(table):
            return jnp.sum(jnp.where(mine, table.astype(F32), 0.0), axis=1, keepdims=True)

        prob_grad = column(last_grad)
        centre = jnp.sum(p * prob_grad, axis=0, keepdims=True)
        score_grad = (p * (prob_grad - centre)).astype(BF16)
        qg_ref[0, :main, at] = (lax.dot_general(
            score_grad, k_ref[0, :, at], (((0,), (0,)), ((), ())), preferred_element_type=F32
        ) * INV_ROOT).astype(BF16)
        kg_ref[0, :, at] = ((
            jnp.dot(score_grad, q_ref[0, :main, at], preferred_element_type=F32)
            + column(last_score) * q_ref[0, main:, at].astype(F32)
        ) * INV_ROOT).astype(BF16)
        mass = column_mass(p.astype(BF16)) + column(last_low)
        vg_ref[0, :, at] = (mass * cot).astype(BF16)


def on_device(
    n_dp, n_mp,
    query_tokens, key_tokens, value_tokens, head_weight, image_cache, text_embed,
    text_pair, image_group, text_group, logit_scale, logit_bias,
):
    _, seq, width = query_tokens.shape
    heads = width // HEAD_DIM
    rows, embed = image_cache.shape
    cw = head_weight.shape[1]
    vmem = pl.BlockSpec(memory_space=pltpu.VMEM)
    any_space = pl.BlockSpec(memory_space=pl.ANY)
    smem = pl.BlockSpec(memory_space=pltpu.SMEM)
    n_q = n_dp // 2
    dma = pltpu.SemaphoreType.DMA
    probs, last_probs, cot, image_grad, text_grad, loss = pl.pallas_call(
        functools.partial(forward_kernel, n_dp, n_mp, heads, embed),
        out_shape=(
            jax.ShapeDtypeStruct((heads, seq, seq - 1), F32),
            jax.ShapeDtypeStruct((seq, HEAD_ROWS), F32),
            jax.ShapeDtypeStruct((1, width), F32),
            jax.ShapeDtypeStruct((rows, embed), F32),
            jax.ShapeDtypeStruct((rows, embed), F32),
            jax.ShapeDtypeStruct((1, rows), F32),
        ),
        in_specs=[any_space] * 4 + [vmem] * 2 + [smem] * 5,
        out_specs=(any_space, vmem, vmem, vmem, vmem, vmem),
        scratch_shapes=[
            pltpu.VMEM(query_tokens.shape, BF16),
            pltpu.VMEM(query_tokens.shape, BF16),
            pltpu.VMEM(query_tokens.shape, BF16),
            pltpu.VMEM(head_weight.shape, BF16),
            pltpu.VMEM((n_dp, n_mp, 2 * rows, embed // 2 + 128), BF16),
            pltpu.VMEM((n_dp, n_mp, 2 * rows, embed // 2 + 128), BF16),
            pltpu.VMEM((n_dp, n_mp * rows, embed), BF16),
            pltpu.VMEM((heads, seq, seq - 1), F32),
            pltpu.VMEM((n_dp, 1, width), F32),
            pltpu.VMEM((n_mp, n_dp, cw), F32),
            pltpu.VMEM((n_dp, n_dp, cw), F32),
            pltpu.VMEM((n_dp, embed), F32),
            pltpu.VMEM((n_dp, 1, width), F32),
            pltpu.VMEM((n_dp, 1, width), F32),
            dma((4,)),
            dma((heads,)),
            dma((n_mp,)), dma((n_mp,)),
            dma((n_q,)), dma((n_q,)),
            dma((n_q,)), dma((n_q,)),
            dma((n_mp,)), dma((n_mp,)),
            dma((n_q,)), dma((n_q,)),
            dma((n_q,)), dma((n_q,)),
            dma((n_dp,)), dma((n_dp,)),
            dma((n_mp,)), dma((n_mp,)),
            dma((n_dp,)), dma((n_dp,)),
            dma((n_dp,)), dma((n_dp,)),
        ],
        compiler_params=pltpu.CompilerParams(
            collective_id=0, has_side_effects=True, vmem_limit_bytes=56 * 2**20),
        name="forward_pairs",
    )(
        query_tokens, key_tokens, value_tokens, head_weight, image_cache, text_embed,
        text_pair, image_group, text_group, logit_scale.reshape(1), logit_bias.reshape(1),
    )

    group = 2 if heads % 2 == 0 else 1
    token = pl.BlockSpec((1, seq, group * HEAD_DIM), lambda h: (0, 0, h))
    whole_rows = pl.BlockSpec((rows, embed), lambda h: (0, 0))
    whole_loss = pl.BlockSpec((1, rows), lambda h: (0, 0))
    query_grad, key_grad, value_grad, image_grad, text_grad, loss = pl.pallas_call(
        functools.partial(backward_kernel, group),
        grid=(heads // group,),
        out_shape=(
            jax.ShapeDtypeStruct(query_tokens.shape, BF16),
            jax.ShapeDtypeStruct(query_tokens.shape, BF16),
            jax.ShapeDtypeStruct(query_tokens.shape, BF16),
            jax.ShapeDtypeStruct((rows, embed), F32),
            jax.ShapeDtypeStruct((rows, embed), F32),
            jax.ShapeDtypeStruct((1, rows), F32),
        ),
        in_specs=[
            token, token, token,
            pl.BlockSpec((group, seq, seq - 1), lambda h: (h, 0, 0)),
            pl.BlockSpec((seq, HEAD_ROWS), lambda h: (0, 0)),
            pl.BlockSpec((1, group * HEAD_DIM), lambda h: (0, h)),
            whole_rows, whole_rows, whole_loss,
        ],
        out_specs=(token, token, token, whole_rows, whole_rows, whole_loss),
        compiler_params=pltpu.CompilerParams(vmem_limit_bytes=56 * 2**20),
        name="attention_back",
    )(query_tokens, key_tokens, value_tokens, probs, last_probs, cot, image_grad, text_grad, loss)
    return query_grad, key_grad, value_grad, image_grad, text_grad, loss.reshape(rows)


def solution(mesh):
    pair_rows = P(("dp", "mp"), None)
    pair = P(("dp", "mp"))
    tokens = P("dp", None, "mp")
    return jax.shard_map(
        functools.partial(on_device, mesh.shape["dp"], mesh.shape["mp"]),
        mesh=mesh,
        in_specs=(
            tokens, tokens, tokens, P("mp", "dp"), pair_rows, pair_rows, pair, pair, pair, P(), P(),
        ),
        out_specs=(tokens, tokens, tokens, pair_rows, pair_rows, pair),
        check_vma=False,
    )
```
